32 devices in a mesh: dp: 8 (over z, x), shard: 4 (over y, core).
Axes of the slice: x: 2, y: 2, z: 4, core: 2. Of those that a mesh axis runs over, the one named last changes fastest.
Arguments:
- tokens: bfloat16 [8192, 2048], P(('dp', 'shard')), may hold values from -6 to 6
- ctx_cotangent: bfloat16 [8192, 1024], P(('dp', 'shard')), may hold values from -0.59765625 to 0.59765625
- latent_cache: bfloat16 [1024, 128, 896], P('dp', 'shard'), may hold values from -300 to 300
- nbr_ids: int32 [128, 2], P(('dp', 'shard')), may hold values from 0 to 1023, as said below
- w_query: bfloat16 [2048, 1024], P('shard'), may hold values from -0.125 to 0.125
- w_key: bfloat16 [896, 1024], P('shard'), may hold values from -0.1875 to 0.1875
- w_value: bfloat16 [896, 1024], P('shard'), may hold values from -0.1875 to 0.1875
Outputs:
- context: bfloat16 [8192, 1024], P(('dp', 'shard'))
- grad_query: float32 [2048, 1024], P(('dp', 'shard'))
- grad_key: float32 [896, 1024], P(('dp', 'shard'))
- grad_value: float32 [896, 1024], P(('dp', 'shard'))
The draws below stay inside these ranges and needn't reach their ends.
Inputs may be any that keep to these rules, and one draw needn't show every extreme that they name: Row r of latent_cache is owned by index r // 128 of dp. Within the 32 ids of one index of dp (its devices' nbr_ids in row-major order), at most 8 name rows of one owner, and in every draw one owner is named exactly 8 times by every index of dp. Ids may repeat.
All inputs are finite; a program needn't handle non-finite values.
Results may differ from the reference program's by a relative error of at most 0.0055.
The reference program's roundings to bfloat16 on the way count: a program that leaves them out, or rounds other values in their place, can miss the bound.
Values may be sent and summed in bfloat16 or wider, within the bound.
No kernel may reach another device: no remote copies, remote signals or barrier semaphores. Data moves between devices by JAX's collectives and lax.ppermute only.
A program may use at most 128 MiB of HBM per device.

```python
import jax
import jax.numpy as jnp
from jax import lax

D = 2048
LAT = 896
HEADS = 8
HEAD_DIM = 128
SPAN = 64
NBR = 2
NT = 128
CH_DEV = 4
ROW_DEV = 128
INNER = 1024
SPANS = 128
TOKENS = 8192
ROWS = 1024
GROUP = 32
CAP = 8
N_DP = 8
N_SHARD = 4


def draw_nbr_ids(key, part):
    owner_count = ROWS // ROW_DEV
    slot_total = owner_count * CAP
    hot_owner = jax.random.randint(jax.random.fold_in(key, 11), (), 0, owner_count)

    def one_group(index):
        group_key = jax.random.fold_in(jax.random.fold_in(key, 12), index)
        first_key, second_key, third_key = jax.random.split(group_key, 3)
        owner_of = jnp.arange(slot_total, dtype=jnp.int32) // CAP
        ranking = jax.random.permutation(first_key, slot_total).astype(jnp.int32)
        ranking = ranking - jnp.where(owner_of == hot_owner, slot_total, 0)
        ordering = jnp.argsort(ranking, stable=True)
        chosen = owner_of[ordering[:GROUP]]
        chosen = jax.random.permutation(second_key, chosen)
        within_row = jax.random.randint(third_key, (GROUP,), 0, ROW_DEV)
        return chosen * ROW_DEV + within_row
    group_count = SPANS * NBR // GROUP
    identities = jax.vmap(one_group)(jnp.arange(group_count))
    return identities.reshape(SPANS, NBR).astype(jnp.int32)


def draw_latent_cache(key, part):
    owner_count = ROWS // ROW_DEV
    base_key, pair_key = jax.random.split(jax.random.fold_in(key, 21), 2)
    values = jnp.clip(jax.random.normal(base_key, (ROWS, NT, LAT), jnp.float32), -6.0, 6.0)
    pairing = jax.random.permutation(pair_key, owner_count)
    owner_of = jnp.arange(ROWS) // ROW_DEV
    column_block = jnp.arange(LAT) * owner_count // LAT
    spiked = pairing[owner_of][:, None] == column_block[None, :]
    values = values * jnp.where(spiked, 4.0, 1.0)[:, None, :]
    return values.astype(jnp.bfloat16)


def raised(result, key, source, target, parts, factor):
    def block_of(axis_at):
        return (jnp.arange(result.shape[axis_at]) // (result.shape[axis_at] // parts)).reshape((-1,) + (1,) * (result.ndim - 1 - axis_at))

    one_side = jax.random.permutation(key, parts)[block_of(target)]
    second = (block_of(target) + parts // 2) % parts
    return jnp.where((block_of(source) == one_side) | (block_of(source) == second), factor * result, result)


def steps_of(stream_key, shape, cuts, least, top_value):
    def one(dim, blocks):
        draws = jax.random.uniform(jax.random.fold_in(jax.random.fold_in(stream_key, 6), dim), (blocks,), jnp.float32, least / len(cuts), top_value / len(cuts))
        return jnp.repeat(jnp.exp(draws), shape[dim] // blocks).reshape((-1,) + (1,) * (len(shape) - dim - 1))

    loudness = one(*cuts[0])
    for cut in cuts[1:]:
        loudness = loudness * one(*cut)
    return loudness


def bell_draw(stream_key, shape, deviation, reach, cuts=(), kind=jnp.bfloat16):
    values = deviation * jax.random.normal(stream_key, shape, jnp.float32)
    if cuts:
        values = values * steps_of(stream_key, shape, cuts, -0.22, 0.18)
    return jnp.clip(values, -reach, reach).astype(kind)


def noise_with(key, dims, deviation, limit, shards, heavy, kind=jnp.bfloat16):
    entries = deviation * jax.random.normal(key, dims, jnp.float32)
    if shards:
        entries = entries * steps_of(key, dims, shards, -0.22, 0.18)
    return jnp.clip(raised(entries, jax.random.fold_in(key, 3), *heavy), -limit, limit).astype(kind)


def setup_inputs(seed: int = 0) -> dict:
    arg_keys = jax.random.split(jax.random.key(seed), 8)
    tokens = noise_with(arg_keys[0], (TOKENS, D), 1.0, 6.0, ((0, 32),), (0, 1, 32, 2.75))
    ctx_cotangent = bell_draw(arg_keys[1], (TOKENS, INNER), 0.1, 0.59765625, ((0, 32),))
    latent_cache = draw_latent_cache(jax.random.fold_in(arg_keys[7], 71), 0)
    nbr_ids = draw_nbr_ids(jax.random.fold_in(arg_keys[7], 71), 0)
    w_query = bell_draw(arg_keys[4], (D, INNER), D ** -0.5, 0.125, ((0, 4),))
    w_key = bell_draw(arg_keys[5], (LAT, INNER), LAT ** -0.5, 0.1875, ((0, 4),))
    w_value = bell_draw(arg_keys[6], (LAT, INNER), LAT ** -0.5, 0.1875, ((0, 4),))
    return dict(tokens=tokens, ctx_cotangent=ctx_cotangent, latent_cache=latent_cache, nbr_ids=nbr_ids, w_query=w_query, w_key=w_key, w_value=w_value)


def attend_block(normed, latent_rows, ctx_grad, w_query, w_key, w_value):
    softmax_scale = HEAD_DIM ** (-0.5)
    query_sum = jnp.dot(normed, w_query, preferred_element_type=jnp.float32)
    queries = (query_sum * softmax_scale).astype(jnp.bfloat16)
    key_rows = jnp.dot(latent_rows, w_key, preferred_element_type=jnp.float32).astype(jnp.bfloat16)
    value_rows = jnp.dot(latent_rows, w_value, preferred_element_type=jnp.float32).astype(jnp.bfloat16)
    query_heads = queries.reshape(CH_DEV, SPAN, HEADS, HEAD_DIM).astype(jnp.float32)
    key_heads = key_rows.reshape(CH_DEV, NBR * NT, HEADS, HEAD_DIM).astype(jnp.float32)
    value_heads = value_rows.reshape(CH_DEV, NBR * NT, HEADS, HEAD_DIM).astype(jnp.float32)
    scores = jnp.einsum('cmhd,cnhd->chmn', query_heads, key_heads)
    highest = lax.optimization_barrier(jnp.max(scores, axis=-1, keepdims=True))
    exp_scores = jnp.exp(scores - highest)
    attn_prob = exp_scores / lax.optimization_barrier(jnp.sum(exp_scores, axis=-1, keepdims=True))
    prob_round = attn_prob.astype(jnp.bfloat16).astype(jnp.float32)
    context = jnp.einsum('chmn,cnhd->cmhd', prob_round, value_heads).astype(jnp.bfloat16)
    grad_heads = ctx_grad.reshape(CH_DEV, SPAN, HEADS, HEAD_DIM).astype(jnp.float32)
    value_grad = jnp.einsum('chmn,cmhd->cnhd', prob_round, grad_heads).astype(jnp.bfloat16)
    prob_grad = jnp.einsum('cmhd,cnhd->chmn', grad_heads, value_heads)
    score_grad = attn_prob * (prob_grad - lax.optimization_barrier(jnp.sum(attn_prob * prob_grad, axis=-1, keepdims=True)))
    score_grad = score_grad.astype(jnp.bfloat16).astype(jnp.float32)
    query_grad = (jnp.einsum('chmn,cnhd->cmhd', score_grad, key_heads) * softmax_scale).astype(jnp.bfloat16)
    key_grad = jnp.einsum('chmn,cmhd->cnhd', score_grad, query_heads).astype(jnp.bfloat16)
    query_grad = query_grad.reshape(CH_DEV * SPAN, INNER)
    key_grad = key_grad.reshape(CH_DEV * NBR * NT, INNER)
    value_grad = value_grad.reshape(CH_DEV * NBR * NT, INNER)
    grad_query = jnp.dot(normed.T, query_grad, preferred_element_type=jnp.float32)
    grad_key = jnp.dot(latent_rows.T, key_grad, preferred_element_type=jnp.float32)
    grad_value = jnp.dot(latent_rows.T, value_grad, preferred_element_type=jnp.float32)
    return (context.reshape(CH_DEV * SPAN, INNER), grad_query, grad_key, grad_value)

def reference(tokens, ctx_cotangent, latent_cache, nbr_ids, w_query, w_key, w_value):
    blocks = N_DP * N_SHARD
    token_blocks = tokens.reshape(blocks, CH_DEV * SPAN, D)
    grad_blocks = ctx_cotangent.reshape(blocks, CH_DEV * SPAN, INNER)
    id_blocks = nbr_ids.reshape(blocks, CH_DEV * NBR)

    def one_block(sums, pieces):
        token_rows, grad_rows, id_rows = pieces
        as_float = token_rows.astype(jnp.float32)
        normed = (as_float * lax.rsqrt(lax.optimization_barrier(jnp.mean(as_float * as_float, axis=-1, keepdims=True)) + 1e-06)).astype(jnp.bfloat16)
        latent_rows = latent_cache[id_rows.astype(jnp.int32)].reshape(CH_DEV * NBR * NT, LAT)
        context, grad_query, grad_key, grad_value = attend_block(normed, latent_rows, grad_rows, w_query, w_key, w_value)
        return ((sums[0] + grad_query, sums[1] + grad_key, sums[2] + grad_value), context)
    start_sums = (jnp.zeros((D, INNER), jnp.float32), jnp.zeros((LAT, INNER), jnp.float32), jnp.zeros((LAT, INNER), jnp.float32))
    sums, contexts = lax.scan(one_block, start_sums, (token_blocks, grad_blocks, id_blocks))
    return (contexts.reshape(TOKENS, INNER), sums[0], sums[1], sums[2])
```

```python
import functools

import jax
import jax.numpy as jnp
from jax import lax
from jax.experimental import pallas as pl
from jax.experimental.pallas import tpu as pltpu
from jax.sharding import PartitionSpec as P

HEAD_DIM = 128
AXES = ("dp", "shard")
LANES = 128
ANY = pl.BlockSpec(memory_space=pl.ANY)
SMEM = pl.BlockSpec(memory_space=pltpu.SMEM)
VMEM = pl.BlockSpec(memory_space=pltpu.VMEM)
VMEM_LIMIT = 56 * 1024 * 1024
F32 = jnp.float32
BF16 = jnp.bfloat16


def lane_cuts(width, shares):
    tiles = width // LANES
    total = sum(shares)
    ends = [0]
    for k in range(1, len(shares) + 1):
        ends.append(round(tiles * sum(shares[:k]) / total) * LANES)
    return [(a, b - a) for a, b in zip(ends, ends[1:]) if b > a]


def serve_kernel(groups, group, slots, owned, cuts, ids, place, cache, *rest):
    outs, (table, sem) = rest[: len(cuts)], rest[len(cuts) :]
    me = place[0]

    def ask(g, carry):
        def scan(i, at):
            row = ids[g * group + i] - me * owned
            mine = jnp.logical_and(row >= 0, row < owned)
            table[at] = jnp.clip(row, 0, owned - 1)
            return jnp.where(mine, at + 1, at)

        at = lax.fori_loop(0, group, scan, g * slots, unroll=True)

        def fill(k, at):
            table[k] = jnp.where(k < at, table[k], 0)
            row = table[k]
            for (start, width), out in zip(cuts, outs):
                pltpu.make_async_copy(
                    cache.at[row, :, pl.ds(start, width)], out.at[k], sem
                ).start()
            return at

        lax.fori_loop(g * slots, g * slots + slots, fill, at)
        return carry

    lax.fori_loop(0, groups, ask, 0)
    for out in outs:
        pltpu.make_async_copy(out, out, sem).wait()


def pick_kernel(group, slots, owned, owners, shards, ids, place, arrived, *rest):
    outs, (count, sem) = rest[:shards], rest[shards:]
    me, shard = place[0], place[1]
    each = group // shards

    def clear(k, carry):
        count[k] = 0
        return carry

    lax.fori_loop(0, owners, clear, 0)

    def locate(i, carry):
        owner = ids[me * group + i] // owned
        at = count[owner]
        count[owner] = at + 1
        count[owners + i] = owner * slots + at
        return carry

    lax.fori_loop(0, group, locate, 0, unroll=8)
    for k in range(shards):
        peer = jnp.bitwise_xor(shard, k)
        for j in range(each):
            at = count[owners + peer * each + j]
            pltpu.make_async_copy(arrived.at[at], outs[k].at[j], sem).start()
    for k in range(shards):
        pltpu.make_async_copy(outs[k], outs[k], sem).wait()


def attend_kernel(parts, shards, heads, scale, *refs):
    pieces, refs = refs[: parts * shards], refs[parts * shards :]
    queries, cotangent, w_key, w_value = refs[:4]
    context, query_grad, key_grad, value_grad, latents = refs[4:9]
    key_rows, value_rows = refs[9:]
    nbr, tokens, _ = pieces[0].shape
    for k in range(shards):
        at = 0
        for j in range(parts):
            piece = pieces[j * shards + k]
            width = piece.shape[2]
            latents[k * nbr * tokens : (k + 1) * nbr * tokens, at : at + width] = piece[
                ...
            ].reshape(nbr * tokens, width)
            at += width
    rows = latents[...]
    key_rows[...] = jnp.dot(rows, w_key[...], preferred_element_type=F32).astype(BF16)
    value_rows[...] = jnp.dot(rows, w_value[...], preferred_element_type=F32).astype(
        BF16
    )
    dot = functools.partial(lax.dot_general, preferred_element_type=F32)
    nt = (((1,), (1,)), ((), ()))
    nn = (((1,), (0,)), ((), ()))
    tn = (((0,), (0,)), ((), ()))
    for h in range(heads):
        cols = slice(h * HEAD_DIM, (h + 1) * HEAD_DIM)
        query, grad = queries[:, cols], cotangent[:, cols]
        key, value = key_rows[:, cols], value_rows[:, cols]
        scores = dot(query, key, nt)
        raised = jnp.exp(scores - jnp.max(scores, axis=-1, keepdims=True))
        prob = raised * (1.0 / jnp.sum(raised, axis=-1, keepdims=True))
        rounded = prob.astype(BF16)
        context[:, cols] = dot(rounded, value, nn).astype(BF16)
        value_grad[:, cols] = dot(rounded, grad, tn).astype(BF16)
        prob_grad = dot(grad, value, nt)
        inner = jnp.sum(prob * prob_grad, axis=-1, keepdims=True)
        score_grad = (prob * (prob_grad - inner)).astype(BF16)
        query_grad[:, cols] = (dot(score_grad, key, nn) * scale).astype(BF16)
        key_grad[:, cols] = dot(score_grad, query, tn).astype(BF16)


def grad_kernel(devices, rows, padded, step, place, left, right, keep, send, total):
    me = place[2]
    odd = jnp.bitwise_and(me, 1) == 1
    half = me >> 1
    width = left.shape[1]
    for at in range(0, width, step):
        size = min(step, width - at)
        total[at : at + size, :] = lax.dot_general(
            left[:, at : at + size],
            right[...],
            (((0,), (0,)), ((), ())),
            preferred_element_type=F32,
        )
    if total.shape[0] > width:
        total[width:, :] = jnp.zeros((total.shape[0] - width, total.shape[1]), F32)
    for d in range(devices // 2):
        even_rows = total[2 * d * rows : 2 * d * rows + padded, :]
        odd_rows = total[(2 * d + 1) * rows : (2 * d + 1) * rows + padded, :]
        at = jnp.bitwise_xor(half, d)
        keep[at] = jnp.where(odd, odd_rows, even_rows)
        send[at] = jnp.where(odd, even_rows, odd_rows).astype(BF16)


def grad_blocks(place, left, right, devices, step):
    width, columns = left.shape[1], right.shape[1]
    rows = width // devices
    padded = -(-rows // 16) * 16
    body = functools.partial(grad_kernel, devices, rows, padded, step)
    return pl.pallas_call(
        body,
        out_shape=(
            jax.ShapeDtypeStruct((devices // 2, padded, columns), F32),
            jax.ShapeDtypeStruct((devices // 2, padded, columns), BF16),
        ),
        in_specs=[SMEM, VMEM, VMEM],
        out_specs=(VMEM, VMEM),
        scratch_shapes=[pltpu.VMEM((width + padded, columns), F32)],
        compiler_params=pltpu.CompilerParams(vmem_limit_bytes=VMEM_LIMIT),
        cost_estimate=pl.CostEstimate(
            flops=2 * width * columns * left.shape[0],
            bytes_accessed=2 * left.size + 2 * right.size + 6 * width * columns,
            transcendentals=0,
        ),
    )(place, left, right)


def swap(value, bit, devices):
    return lax.ppermute(value, AXES, [(i, i ^ bit) for i in range(devices)])


def body(tokens, ctx_cotangent, latent_cache, nbr_ids, w_query, w_key, w_value):
    owners, shards = lax.axis_size("dp"), lax.axis_size("shard")
    devices = owners * shards
    owned, slice_tokens, latent = latent_cache.shape
    spans, nbr = nbr_ids.shape
    each = spans * nbr
    group = each * shards
    slots = 2 * group // owners
    inner = w_query.shape[1]
    heads = inner // HEAD_DIM
    scale = HEAD_DIM**-0.5
    span = tokens.shape[0] // spans
    dp, shard = lax.axis_index("dp"), lax.axis_index("shard")
    place = jnp.stack([dp, shard, dp * shards + shard]).astype(jnp.int32)

    ids = lax.all_to_all(
        jnp.broadcast_to(nbr_ids.reshape(1, each), (devices, each)),
        AXES,
        split_axis=0,
        concat_axis=0,
        tiled=True,
    ).reshape(-1)

    key_full = lax.all_gather(w_key, "shard", axis=0, tiled=True)
    value_full = lax.all_gather(w_value, "shard", axis=0, tiled=True)
    query_full = lax.all_gather(w_query, "shard", axis=0, tiled=True)

    cuts = lane_cuts(latent, (3, 3, 1))
    served = pl.pallas_call(
        functools.partial(serve_kernel, owners, group, slots, owned, cuts),
        out_shape=[
            jax.ShapeDtypeStruct((owners * slots, slice_tokens, width), BF16)
            for _, width in cuts
        ],
        in_specs=[SMEM, SMEM, ANY],
        out_specs=[ANY] * len(cuts),
        scratch_shapes=[
            pltpu.SMEM((owners * slots + 1,), jnp.int32),
            pltpu.SemaphoreType.DMA,
        ],
    )(ids, place, latent_cache)

    pieces = []
    for (_, width), rows in zip(cuts, served):
        arrived = lax.all_to_all(rows, "dp", split_axis=0, concat_axis=0, tiled=True)
        picked = pl.pallas_call(
            functools.partial(pick_kernel, group, slots, owned, owners, shards),
            out_shape=[
                jax.ShapeDtypeStruct((each, slice_tokens, width), BF16)
                for _ in range(shards)
            ],
            in_specs=[SMEM, SMEM, ANY],
            out_specs=[ANY] * shards,
            scratch_shapes=[
                pltpu.SMEM((owners + group,), jnp.int32),
                pltpu.SemaphoreType.DMA,
            ],
        )(ids, place, arrived)
        pieces += [
            piece if k == 0 else swap(piece, k, devices)
            for k, piece in enumerate(picked)
        ]

    as_float = tokens.astype(F32)
    normed = (
        as_float
        * lax.rsqrt(jnp.mean(as_float * as_float, axis=-1, keepdims=True) + 1e-06)
    ).astype(BF16)
    query_sum = jnp.dot(normed, query_full, preferred_element_type=F32)
    queries = (query_sum * scale).astype(BF16)

    keys = nbr * shards * slice_tokens
    piece_specs = [
        pl.BlockSpec((nbr, slice_tokens, piece.shape[2]), lambda c: (c, 0, 0))
        for piece in pieces
    ]
    by_span = pl.BlockSpec((span, inner), lambda c: (c, 0))
    by_keys = pl.BlockSpec((keys, inner), lambda c: (c, 0))
    whole = pl.BlockSpec((latent, inner), lambda c: (0, 0))
    context, query_grad, key_grad, value_grad, latents = pl.pallas_call(
        functools.partial(attend_kernel, len(cuts), shards, heads, scale),
        grid=(spans,),
        out_shape=(
            jax.ShapeDtypeStruct((spans * span, inner), BF16),
            jax.ShapeDtypeStruct((spans * span, inner), BF16),
            jax.ShapeDtypeStruct((spans * keys, inner), BF16),
            jax.ShapeDtypeStruct((spans * keys, inner), BF16),
            jax.ShapeDtypeStruct((spans * keys, latent), BF16),
        ),
        in_specs=piece_specs + [by_span, by_span, whole, whole],
        out_specs=(
            by_span,
            by_span,
            by_keys,
            by_keys,
            pl.BlockSpec((keys, latent), lambda c: (c, 0)),
        ),
        scratch_shapes=[pltpu.VMEM((keys, inner), BF16)] * 2,
        compiler_params=pltpu.CompilerParams(vmem_limit_bytes=VMEM_LIMIT),
        cost_estimate=pl.CostEstimate(
            flops=4 * spans * keys * inner * (latent + 3 * span),
            bytes_accessed=2 * spans * keys * (2 * inner + 2 * latent),
            transcendentals=spans * span * keys * heads,
        ),
    )(*pieces, queries, ctx_cotangent, key_full, value_full)

    low = 1 << (owners.bit_length() - 1) // 2
    lengths = dict(z=owners // low, x=low, y=shards // 2)
    bits = dict(z=low * shards, x=shards, y=2)

    def scatter_sum(left, right, order):
        keep, send = grad_blocks(place, left, right, devices, 512)
        total = keep + swap(send, 1, devices).astype(F32)
        total = total.reshape(lengths["z"], lengths["x"], lengths["y"], *keep.shape[1:])
        for name in order:
            axis = "zxy".index(name)
            cut = lambda k: lax.slice_in_dim(total, k, k + 1, axis=axis)
            came = [
                swap(cut(k).astype(BF16), k * bits[name], devices)
                for k in range(1, lengths[name])
            ]
            total = sum((part.astype(F32) for part in came), cut(0))
        return total.reshape(keep.shape[1:])[: left.shape[1] // devices]

    grad_value = scatter_sum(latents, value_grad, "zyx")
    grad_query = scatter_sum(normed, query_grad, "xyz")
    grad_key = scatter_sum(latents, key_grad, "yxz")
    return context, grad_query, grad_key, grad_value


def solution(mesh):
    rows = P(AXES, None)
    by_shard = P("shard", None)
    return jax.shard_map(
        body,
        mesh=mesh,
        in_specs=(rows, rows, P("dp", "shard", None), rows)
        + (by_shard, by_shard, by_shard),
        out_specs=(rows, rows, rows, rows),
        check_vma=False,
    )
```

```python
import functools

import jax
import jax.numpy as jnp
from jax import lax
from jax.experimental import pallas as pl
from jax.experimental.pallas import tpu as pltpu
from jax.sharding import PartitionSpec as P

HEAD_DIM = 128
AXES = ("dp", "shard")
LANES = 128
ANY = pl.BlockSpec(memory_space=pl.ANY)
SMEM = pl.BlockSpec(memory_space=pltpu.SMEM)
VMEM = pl.BlockSpec(memory_space=pltpu.VMEM)
VMEM_LIMIT = 56 * 1024 * 1024
F32 = jnp.float32
BF16 = jnp.bfloat16


def lane_cuts(width, shares):
    tiles = width // LANES
    total = sum(shares)
    ends = [0]
    for k in range(1, len(shares) + 1):
        ends.append(round(tiles * sum(shares[:k]) / total) * LANES)
    return [(a, b - a) for a, b in zip(ends, ends[1:]) if b > a]


def serve_kernel(owners, slots, owned, start, after, ids, place, cache, *rest):
    rest = rest[after:]
    outs, (table, sem) = rest[:owners], rest[owners:]
    me = place[0]
    shards, each = ids.shape[0] // owners, ids.shape[1]
    width = outs[0].shape[2]
    for k in range(owners):
        asking = jnp.bitwise_xor(me, k)
        base = k * slots

        def scan(s, at):
            for i in range(each):
                row = ids[asking * shards + s, i] - me * owned
                mine = jnp.logical_and(row >= 0, row < owned)
                table[at] = jnp.clip(row, 0, owned - 1)
                at = jnp.where(mine, at + 1, at)
            return at

        at = lax.fori_loop(0, shards, scan, base)
        for j in range(slots):
            row = jnp.where(base + j < at, table[base + j], 0)
            pltpu.make_async_copy(
                cache.at[row, :, pl.ds(start, width)], outs[k].at[j], sem
            ).start()
    for out in outs:
        pltpu.make_async_copy(out, out, sem).wait()


def pick_kernel(owners, shards, owned, after, ids, place, *rest):
    arrived, rest = rest[:owners], rest[after:]
    outs = rest[owners : owners + shards]
    count, sem = rest[owners + shards :]
    me, shard = place[0], place[1]
    each = ids.shape[1]
    for k in range(owners):
        count[k] = 0

    def locate(s, carry):
        for i in range(each):
            owner = ids[me * shards + s, i] // owned
            at = count[owner]
            count[owner] = at + 1
            count[owners + s * each + i] = at
        return carry

    lax.fori_loop(0, shards, locate, 0)
    for k in range(shards):
        peer = jnp.bitwise_xor(shard, k)
        for j in range(each):
            source = jnp.bitwise_xor(ids[me * shards + peer, j] // owned, me)
            at = count[owners + peer * each + j]
            for n in range(owners):

                @pl.when(source == n)
                def _(n=n, k=k, j=j, at=at):
                    pltpu.make_async_copy(
                        arrived[n].at[at], outs[k].at[j], sem
                    ).start()

    for out in outs:
        pltpu.make_async_copy(out, out, sem).wait()


def concat_kernel(after, *refs):
    out, at = refs[-1], 0
    for ref in refs[: len(refs) - 1 - after]:
        out[at : at + ref.shape[0], :] = ref[...]
        at += ref.shape[0]


def place_blocks(total, rows, place, turn, first, targets):
    me = place[2]
    odd = jnp.bitwise_and(me, 1) == 1
    half = me >> 1
    for d in range(first):
        rel = jnp.bitwise_xor(half, d)
        for order, keep, send, source, into, size in targets:
            even_at = 2 * d * rows + source
            odd_at = even_at + rows
            even_rows = total[even_at : even_at + size, :]
            odd_rows = total[odd_at : odd_at + size, :]
            at = turn(rel, order)
            keep[at, into : into + size, :] = jnp.where(odd, odd_rows, even_rows)
            send[at, into : into + size, :] = jnp.where(odd, even_rows, odd_rows).astype(
                BF16
            )


def combine_kernel(counts, split, after, *refs):
    inputs, outs = [], refs[sum(counts) + after :]
    for count in counts:
        inputs.append(refs[:count])
        refs = refs[count:]
    each = inputs[0][0].shape[0] // split
    for k in range(split):
        at = 0
        for parts in inputs:
            rows = parts[0].shape[1]

            def one(i, carry, k=k, at=at, rows=rows, parts=parts):
                total = parts[0][k * each + i]
                for part in parts[1:]:
                    total = total + part[k * each + i].astype(F32)
                outs[k][i, at : at + rows, :] = total.astype(outs[k].dtype)
                return carry

            lax.fori_loop(0, each, one, 0)
            at += rows


def combine(groups, split, after=()):
    lead, _, columns = groups[0][0].shape
    rows = sum(group[0].shape[1] for group in groups)
    shape = (lead // split, rows, columns)
    flat = [array for group in groups for array in group]
    body = functools.partial(
        combine_kernel, [len(group) for group in groups], split, len(after)
    )
    moved = sum(array.size * array.dtype.itemsize for array in flat)
    keep, *sends = pl.pallas_call(
        body,
        out_shape=[jax.ShapeDtypeStruct(shape, F32)]
        + [jax.ShapeDtypeStruct(shape, BF16)] * (split - 1),
        in_specs=[VMEM] * len(flat) + [ANY] * len(after),
        out_specs=[VMEM] * split,
        compiler_params=pltpu.CompilerParams(vmem_limit_bytes=2 * moved + (4 << 20)),
    )(*flat, *after)
    return keep, sends


def attend_kernel(parts, shards, heads, scale, devices, spans, turn, *refs):
    pieces, refs = refs[: parts * shards], refs[parts * shards :]
    place, queries, cotangent, normed_t, w_key, w_value = refs[:6]
    context, keep_v, send_v, keep_p, send_p, keep_r, send_r = refs[6:13]
    key_rows, value_rows, scores, prob_grads, prob_rounds, score_grads = refs[13:19]
    latents_t, query_grad, key_grad, value_grad, total_v, total_k, total_q = refs[19:]
    nbr, tokens, _ = pieces[0].shape
    step = pl.program_id(0)
    rows = jnp.concatenate(
        [
            jnp.concatenate(
                [
                    pieces[j * shards + k][...].reshape(nbr * tokens, -1)
                    for j in range(parts)
                ],
                axis=1,
            )
            for k in range(shards)
        ],
        axis=0,
    )
    keys, latent = rows.shape
    span, inner = queries.shape
    latents_t[step] = rows.T
    key_rows[...] = jnp.dot(rows, w_key[...], preferred_element_type=F32).astype(BF16)
    value_rows[...] = jnp.dot(rows, w_value[...], preferred_element_type=F32).astype(
        BF16
    )
    dot = functools.partial(lax.dot_general, preferred_element_type=F32)
    nt = (((1,), (1,)), ((), ()))
    nn = (((1,), (0,)), ((), ()))
    tn = (((0,), (0,)), ((), ()))
    of_keys = pl.ds(pl.multiple_of(step * keys, keys), keys)
    of_span = pl.ds(pl.multiple_of(step * span, span), span)

    def at_head(h):
        return slice(h * span, (h + 1) * span), slice(h * HEAD_DIM, (h + 1) * HEAD_DIM)

    for h in range(heads):
        stacked, cols = at_head(h)
        scores[stacked, :] = dot(queries[:, cols], key_rows[:, cols], nt)
        prob_grads[stacked, :] = dot(cotangent[:, cols], value_rows[:, cols], nt)
    for h in range(heads):
        stacked, _ = at_head(h)
        score = scores[stacked, :]
        raised = jnp.exp(score - jnp.max(score, axis=-1, keepdims=True))
        prob = raised * (1.0 / jnp.sum(raised, axis=-1, keepdims=True))
        prob_rounds[stacked, :] = prob.astype(BF16)
        prob_grad = prob_grads[stacked, :]
        inner_sum = jnp.sum(prob * prob_grad, axis=-1, keepdims=True)
        score_grads[stacked, :] = (prob * (prob_grad - inner_sum)).astype(BF16)
    for h in range(heads):
        stacked, cols = at_head(h)
        prob, score_grad = prob_rounds[stacked, :], score_grads[stacked, :]
        context[:, cols] = dot(prob, value_rows[:, cols], nn).astype(BF16)
        value_grad[of_keys, cols] = dot(prob, cotangent[:, cols], tn).astype(BF16)
        query_grad[of_span, cols] = (
            dot(score_grad, key_rows[:, cols], nn) * scale
        ).astype(BF16)
        key_grad[of_keys, cols] = dot(score_grad, queries[:, cols], tn).astype(BF16)

    @pl.when(step == spans - 1)
    def _():
        across = jnp.concatenate([latents_t[c] for c in range(spans)], axis=1)
        of_v, of_p, of_r = (0, keep_v, send_v), (1, keep_p, send_p), (2, keep_r, send_r)
        rows_k, rows_q = keep_v.shape[1], total_q.shape[0] // devices
        shared = keep_p.shape[1] - rows_k
        for total, grad, target in ((total_v, value_grad, of_v), (total_k, key_grad, of_p)):
            total[:latent, :] = dot(across, grad[...], nn)
            total[latent:, :] = jnp.zeros((total.shape[0] - latent, inner), F32)
            place_blocks(
                total, latent // devices, place, turn, devices // 2, [target + (0, 0, rows_k)]
            )
        total_q[...] = dot(normed_t[...], query_grad[...], nn)
        targets = [of_r + (shared, 0, rows_q - shared)]
        if shared:
            targets.append(of_p + (0, rows_k, shared))
        place_blocks(total_q, rows_q, place, turn, devices // 2, targets)


def swap(value, bit, devices):
    return lax.ppermute(value, AXES, [(i, i ^ bit) for i in range(devices)])


def body(tokens, ctx_cotangent, latent_cache, nbr_ids, w_query, w_key, w_value):
    owners, shards = lax.axis_size("dp"), lax.axis_size("shard")
    devices = owners * shards
    owned, slice_tokens, latent = latent_cache.shape
    spans, nbr = nbr_ids.shape
    each = spans * nbr
    group = each * shards
    slots = 2 * group // owners
    inner = w_query.shape[1]
    heads = inner // HEAD_DIM
    scale = HEAD_DIM**-0.5
    span = tokens.shape[0] // spans
    dp, shard = lax.axis_index("dp"), lax.axis_index("shard")
    place = jnp.stack([dp, shard, dp * shards + shard]).astype(jnp.int32)

    ids = lax.all_to_all(
        jnp.broadcast_to(nbr_ids.reshape(1, each), (devices, each)),
        AXES,
        split_axis=0,
        concat_axis=0,
        tiled=True,
    )
    as_float = tokens.astype(F32)
    normed = (
        as_float
        * lax.rsqrt(jnp.mean(as_float * as_float, axis=-1, keepdims=True) + 1e-06)
    ).astype(BF16)

    pieces = []
    cuts = lane_cuts(latent, (3, 3, 1))
    before = []
    for turn_at, (start, width) in enumerate(cuts):
        served = pl.pallas_call(
            functools.partial(serve_kernel, owners, slots, owned, start, len(before)),
            out_shape=[jax.ShapeDtypeStruct((slots, slice_tokens, width), BF16)]
            * owners,
            in_specs=[SMEM, SMEM, ANY] + [ANY] * len(before),
            out_specs=[VMEM] * owners,
            scratch_shapes=[
                pltpu.SMEM((owners * slots + 1,), jnp.int32),
                pltpu.SemaphoreType.DMA,
            ],
            compiler_params=pltpu.CompilerParams(vmem_limit_bytes=16 << 20),
        )(ids, place, latent_cache, *before)
        arrived = [
            part if k == 0 else swap(part, k * shards, devices)
            for k, part in enumerate(served)
        ]
        if turn_at == 0:
            heights = [w.shape[0] for w in (w_query, w_key, w_value)]
            weights = pl.pallas_call(
                functools.partial(concat_kernel, 1),
                out_shape=jax.ShapeDtypeStruct((sum(heights), inner), BF16),
                in_specs=[VMEM] * 3 + [ANY],
                out_specs=VMEM,
                compiler_params=pltpu.CompilerParams(vmem_limit_bytes=16 << 20),
            )(w_query, w_key, w_value, served[0])
            before = [weights]
            weights = lax.all_gather(weights, "shard", axis=0)
            a, b = heights[0], heights[0] + heights[1]
            query_full = weights[:, :a].reshape(-1, inner)
            key_full = weights[:, a:b].reshape(-1, inner)
            value_full = weights[:, b:].reshape(-1, inner)
            query_sum = jnp.dot(normed, query_full, preferred_element_type=F32)
            queries = (query_sum * scale).astype(BF16)
            normed_t = normed.T
        else:
            before = [served[0]]
        ready = []
        if turn_at == len(cuts) - 1:
            ready = [queries, key_full, value_full, normed_t]
        picked = pl.pallas_call(
            functools.partial(pick_kernel, owners, shards, owned, len(ready)),
            out_shape=[jax.ShapeDtypeStruct((each, slice_tokens, width), BF16)]
            * shards,
            in_specs=[SMEM, SMEM] + [ANY] * (owners + len(ready)),
            out_specs=[VMEM] * shards,
            scratch_shapes=[
                pltpu.SMEM((owners + group,), jnp.int32),
                pltpu.SemaphoreType.DMA,
            ],
            compiler_params=pltpu.CompilerParams(vmem_limit_bytes=16 << 20),
        )(ids, place, *arrived, *ready)
        pieces += [
            piece if k == 0 else swap(piece, k, devices)
            for k, piece in enumerate(picked)
        ]

    keys = nbr * shards * slice_tokens
    width_q = tokens.shape[1]
    by_span = pl.BlockSpec((span, inner), lambda c: (c, 0))

    def fixed(*shape):
        return pl.BlockSpec(
            shape, lambda c: (0,) * len(shape), pipeline_mode=pl.Buffered(1)
        )

    low = 1 << (owners.bit_length() - 1) // 2
    length = dict(z=owners // low, x=low, y=shards // 2)
    bit = dict(z=low * shards, x=shards, y=2)
    orders = ("zyx", "yxz", "xyz")

    def turn(rel, which):
        at = dict(
            y=rel % length["y"],
            x=rel // length["y"] % length["x"],
            z=rel // (length["y"] * length["x"]),
        )
        first, second, third = orders[which]
        return (at[first] * length[second] + at[second]) * length[third] + at[third]

    rows_k = -(-latent // devices // 16) * 16
    rows_q = width_q // devices
    shared = max(0, (rows_k + rows_q) // 32 * 16 - rows_k)
    blocks, block_specs = [], []
    for rows in (rows_k, rows_k + shared, rows_q - shared):
        for kind in (F32, BF16):
            shape = (devices // 2, rows, inner)
            blocks.append(jax.ShapeDtypeStruct(shape, kind))
            block_specs.append(fixed(*shape))
    spare = rows_k
    context, *blocks = pl.pallas_call(
        functools.partial(
            attend_kernel,
            len(pieces) // shards,
            shards,
            heads,
            scale,
            devices,
            spans,
            turn,
        ),
        grid=(spans,),
        out_shape=[jax.ShapeDtypeStruct((spans * span, inner), BF16)] + blocks,
        in_specs=[
            pl.BlockSpec((nbr, slice_tokens, piece.shape[2]), lambda c: (c, 0, 0))
            for piece in pieces
        ]
        + [SMEM, by_span, by_span, fixed(width_q, spans * span)]
        + [fixed(latent, inner)] * 2,
        out_specs=[by_span] + block_specs,
        scratch_shapes=[pltpu.VMEM((keys, inner), BF16)] * 2
        + [pltpu.VMEM((heads * span, keys), F32)] * 2
        + [pltpu.VMEM((heads * span, keys), BF16)] * 2
        + [
            pltpu.VMEM((spans, latent, keys), BF16),
            pltpu.VMEM((spans * span, inner), BF16),
        ]
        + [pltpu.VMEM((spans * keys, inner), BF16)] * 2
        + [pltpu.VMEM((latent + spare, inner), F32)] * 2
        + [pltpu.VMEM((width_q, inner), F32)],
        compiler_params=pltpu.CompilerParams(vmem_limit_bytes=VMEM_LIMIT),
        cost_estimate=pl.CostEstimate(
            flops=2 * inner * (4 * spans * keys * (latent + 2 * span) + tokens.size),
            bytes_accessed=12 * (2 * latent + width_q) * inner,
            transcendentals=spans * span * keys * heads,
        ),
    )(*pieces, place, queries, ctx_cotangent, normed_t, key_full, value_full)

    def travel(sends, axis):
        return [swap(part, k * bit[axis], devices) for k, part in enumerate(sends, 1)]

    keep_v, send_v, keep_p, send_p, keep_r, send_r = blocks
    came_v, came_p, came_r = (swap(s, 1, devices) for s in (send_v, send_p, send_r))
    keep_v, sends = combine([[keep_v, came_v]], length["z"])
    came_v = travel(sends, "z")
    keep_p, sends = combine([[keep_p, came_p]], length["y"], sends[:1])
    came_p = travel(sends, "y")
    keep_r, sends = combine([[keep_r, came_r]], length["x"], sends[:1])
    came_r = travel(sends, "x")
    keep_p, sends = combine([[keep_p, *came_p]], length["x"], sends[:1])
    came_p = travel(sends, "x")
    keep_r, sends = combine([[keep_r, *came_r]], length["y"], sends[:1])
    came_r = travel(sends, "y")
    keep_v, sends = combine([[keep_v, *came_v]], length["y"], sends[:1])
    came_v = travel(sends, "y")
    keep, sends = combine(
        [[keep_p, *came_p], [keep_r, *came_r]], length["z"], sends[:1]
    )
    came = travel(sends, "z")
    keep_v, sends = combine([[keep_v, *came_v]], length["x"], sends[:1])
    came_v = travel(sends, "x")

    def whole_sum(parts):
        return sum((part[0].astype(F32) for part in parts[1:]), parts[0][0])

    grad_value = whole_sum([keep_v, *came_v])[: latent // devices]
    rest = whole_sum([keep, *came])
    grad_key, grad_query = rest[: latent // devices], rest[rows_k:]
    return context, grad_query, grad_key, grad_value


def solution(mesh):
    rows = P(AXES, None)
    by_shard = P("shard", None)
    return jax.shard_map(
        body,
        mesh=mesh,
        in_specs=(rows, rows, P("dp", "shard", None), rows)
        + (by_shard, by_shard, by_shard),
        out_specs=(rows, rows, rows, rows),
        check_vma=False,
    )
```

```python
import functools

import jax
import jax.numpy as jnp
from jax import lax
from jax.experimental import pallas as pl
from jax.experimental.pallas import tpu as pltpu
from jax.sharding import PartitionSpec as P

HEAD_DIM = 128
AXES = ("dp", "shard")
LANES = 128
ANY = pl.BlockSpec(memory_space=pl.ANY)
HBM = pl.BlockSpec(memory_space=pltpu.HBM)
SMEM = pl.BlockSpec(memory_space=pltpu.SMEM)
VMEM = pl.BlockSpec(memory_space=pltpu.VMEM)
F32 = jnp.float32
BF16 = jnp.bfloat16


def lane_cuts(width, shares):
    tiles = width // LANES
    total = sum(shares)
    ends = [0]
    for k in range(1, len(shares) + 1):
        ends.append(round(tiles * sum(shares[:k]) / total) * LANES)
    return [(a, b - a) for a, b in zip(ends, ends[1:]) if b > a]


def serve_kernel(owners, slots, owned, start, lay, after, ids, place, cache, *rest):
    parts, (*outs, table, sem) = rest[:lay], rest[lay + after :]
    if lay:
        *outs, joined = outs
        at = 0
        for part in parts:
            size = part.shape[0]
            pltpu.make_async_copy(part, joined.at[pl.ds(at, size)], sem).start()
            at += size
    me = place[0]
    shards, each = ids.shape[0] // owners, ids.shape[1]
    width = outs[0].shape[2]
    for k in range(owners):
        asking = jnp.bitwise_xor(me, k)
        base = k * slots

        def scan(s, at):
            for i in range(each):
                row = ids[asking * shards + s, i] - me * owned
                mine = jnp.logical_and(row >= 0, row < owned)
                table[at] = jnp.clip(row, 0, owned - 1)
                at = jnp.where(mine, at + 1, at)
            return at

        at = lax.fori_loop(0, shards, scan, base)
        for j in range(slots):
            row = jnp.where(base + j < at, table[base + j], 0)
            into = outs[0].at[asking * slots + j] if len(outs) == 1 else outs[k].at[j]
            pltpu.make_async_copy(
                cache.at[row, :, pl.ds(start, width)], into, sem
            ).start()
    for out in outs + [joined] if lay else outs:
        pltpu.make_async_copy(out, out, sem).wait()


def pick_kernel(owners, slots, shards, owned, lanes, after, ids, place, *rest):
    arrived, rest = rest[:lanes], rest[lanes + after :]
    outs = rest[:shards]
    count, sem = rest[shards:]
    me, shard = place[0], place[1]
    each = ids.shape[1]
    for k in range(owners):
        count[k] = 0

    def locate(s, carry):
        for i in range(each):
            owner = ids[me * shards + s, i] // owned
            at = count[owner]
            count[owner] = at + 1
            count[owners + s * each + i] = at
        return carry

    lax.fori_loop(0, shards, locate, 0)
    for k in range(shards):
        peer = jnp.bitwise_xor(shard, k)
        for j in range(each):
            owner = ids[me * shards + peer, j] // owned
            at = count[owners + peer * each + j]
            if lanes == 1:
                pltpu.make_async_copy(
                    arrived[0].at[owner * slots + at], outs[k].at[j], sem
                ).start()
                continue
            for n in range(owners):

                @pl.when(jnp.bitwise_xor(owner, me) == n)
                def _(n=n, k=k, j=j, at=at):
                    pltpu.make_async_copy(
                        arrived[n].at[at], outs[k].at[j], sem
                    ).start()

    for out in outs:
        pltpu.make_async_copy(out, out, sem).wait()


def place_blocks(total, rows, place, turn, pairs, targets):
    me = place[2]
    odd = jnp.bitwise_and(me, 1) == 1
    half = me >> 1
    for d in pairs:
        rel = jnp.bitwise_xor(half, d)
        for order, keep, send, source, into, size in targets:
            even_at = 2 * (d - pairs[0]) * rows + source
            odd_at = even_at + rows
            even_rows = total[even_at : even_at + size, :]
            odd_rows = total[odd_at : odd_at + size, :]
            at = turn(rel, order)
            keep[at, into : into + size, :] = jnp.where(odd, odd_rows, even_rows).astype(
                BF16
            )
            send[at, into : into + size, :] = jnp.where(odd, even_rows, odd_rows).astype(
                BF16
            )


def combine_kernel(counts, split, after, *refs):
    inputs, outs = [], refs[sum(counts) + after :]
    for count in counts:
        inputs.append(refs[:count])
        refs = refs[count:]
    each = inputs[0][0].shape[0] // split
    for k in range(split):
        at = 0
        for parts in inputs:
            rows = parts[0].shape[1]

            def one(i, carry, k=k, at=at, rows=rows, parts=parts):
                total = parts[0][k * each + i].astype(F32)
                for part in parts[1:]:
                    total = total + part[k * each + i].astype(F32)
                outs[k][i, at : at + rows, :] = total.astype(outs[k].dtype)
                return carry

            lax.fori_loop(0, each, one, 0)
            at += rows


def finish_kernel(first, rows_k, *refs):
    ends, (grad_query, grad_key, grad_value) = refs[:-3], refs[-3:]

    def total(parts, at, size):
        result = parts[0][0, at : at + size, :]
        for part in parts[1:]:
            result = result + part[0, at : at + size, :].astype(F32)
        return result

    exact = grad_key.shape[0]
    grad_value[...] = total(ends[:first], 0, rows_k)[:exact]
    grad_key[...] = total(ends[first:], 0, rows_k)[:exact]
    grad_query[...] = total(ends[first:], rows_k, grad_query.shape[0])


def combine(groups, split, after=()):
    lead, _, columns = groups[0][0].shape
    rows = sum(group[0].shape[1] for group in groups)
    shape = (lead // split, rows, columns)
    flat = [array for group in groups for array in group]
    body = functools.partial(
        combine_kernel, [len(group) for group in groups], split, len(after)
    )
    moved = sum(array.size * array.dtype.itemsize for array in flat)
    keep, *sends = pl.pallas_call(
        body,
        out_shape=[jax.ShapeDtypeStruct(shape, F32)]
        + [jax.ShapeDtypeStruct(shape, BF16)] * (split - 1),
        in_specs=[VMEM] * len(flat) + [ANY] * len(after),
        out_specs=[VMEM] * split,
        compiler_params=pltpu.CompilerParams(vmem_limit_bytes=2 * moved + (4 << 20)),
    )(*flat, *after)
    return keep, sends


def attend_kernel(parts, shards, heads, scale, devices, spans, turn, *refs):
    pieces, refs = refs[: parts * shards], refs[parts * shards :]
    place, queries, cotangent, normed_hbm, weights, context = refs[:6]
    results, refs = refs[6:12], refs[12:]
    key_rows, value_rows, scores, prob_grads, prob_rounds, score_grads = refs[:6]
    latents_t, query_grad, key_grad, value_grad, total_v, total_k, total_q = refs[6:13]
    keep_v, send_v, keep_p, send_p, keep_r, send_r = staged = refs[13:19]
    w_key, w_value, normed_t, weight_sem, normed_sem, out_sem = refs[19:]
    nbr, tokens, _ = pieces[0].shape
    step = pl.program_id(0)
    rows = jnp.concatenate(
        [
            jnp.concatenate(
                [
                    pieces[j * shards + k][...].reshape(nbr * tokens, -1)
                    for j in range(parts)
                ],
                axis=1,
            )
            for k in range(shards)
        ],
        axis=0,
    )
    keys, latent = rows.shape
    span, inner = queries.shape
    latents_t[step] = rows.T
    each = w_key.shape[0] // shards
    skipped = weights.shape[1] - 2 * each

    @pl.when(step == 0)
    def _():
        pltpu.make_async_copy(normed_hbm, normed_t, normed_sem).start()
        for which, held_weights in enumerate((w_key, w_value)):
            for k in range(shards):
                pltpu.make_async_copy(
                    weights.at[k, pl.ds(skipped + which * each, each)],
                    held_weights.at[pl.ds(k * each, each)],
                    weight_sem.at[which],
                ).start()
        for which, held_weights in enumerate((w_key, w_value)):
            pltpu.make_async_copy(
                held_weights, held_weights, weight_sem.at[which]
            ).wait()

    key_rows[...] = jnp.dot(rows, w_key[...], preferred_element_type=F32).astype(BF16)
    value_rows[...] = jnp.dot(rows, w_value[...], preferred_element_type=F32).astype(
        BF16
    )
    dot = functools.partial(lax.dot_general, preferred_element_type=F32)
    nt = (((1,), (1,)), ((), ()))
    nn = (((1,), (0,)), ((), ()))
    tn = (((0,), (0,)), ((), ()))
    of_keys = pl.ds(pl.multiple_of(step * keys, keys), keys)
    of_span = pl.ds(pl.multiple_of(step * span, span), span)

    def at_head(h):
        return slice(h * span, (h + 1) * span), slice(h * HEAD_DIM, (h + 1) * HEAD_DIM)

    for h in range(heads):
        stacked, cols = at_head(h)
        scores[stacked, :] = dot(queries[:, cols], key_rows[:, cols], nt)
        prob_grads[stacked, :] = dot(cotangent[:, cols], value_rows[:, cols], nt)
    for h in range(heads):
        stacked, _ = at_head(h)
        score = scores[stacked, :]
        raised = jnp.exp(score - jnp.max(score, axis=-1, keepdims=True))
        prob = raised * (1.0 / jnp.sum(raised, axis=-1, keepdims=True))
        prob_rounds[stacked, :] = prob.astype(BF16)
        prob_grad = prob_grads[stacked, :]
        inner_sum = jnp.sum(prob * prob_grad, axis=-1, keepdims=True)
        score_grads[stacked, :] = (prob * (prob_grad - inner_sum)).astype(BF16)
    for h in range(heads):
        stacked, cols = at_head(h)
        prob, score_grad = prob_rounds[stacked, :], score_grads[stacked, :]
        context[:, cols] = dot(prob, value_rows[:, cols], nn).astype(BF16)
        value_grad[of_keys, cols] = dot(prob, cotangent[:, cols], tn).astype(BF16)
        query_grad[of_span, cols] = (
            dot(score_grad, key_rows[:, cols], nn) * scale
        ).astype(BF16)
        key_grad[of_keys, cols] = dot(score_grad, queries[:, cols], tn).astype(BF16)

    @pl.when(step == spans - 1)
    def _():
        across = jnp.concatenate([latents_t[c] for c in range(spans)], axis=1)
        of_v, of_p, of_r = (0, keep_v, send_v), (1, keep_p, send_p), (2, keep_r, send_r)
        rows_k, rows_q = keep_v.shape[1], normed_t.shape[0] // devices
        shared = keep_p.shape[1] - rows_k

        def write(first):
            for n in (first, first + 1):
                pltpu.make_async_copy(staged[n], results[n], out_sem.at[n]).start()

        for total, grad, target in ((total_v, value_grad, of_v), (total_k, key_grad, of_p)):
            total[:latent, :] = dot(across, grad[...], nn)
            total[latent:, :] = jnp.zeros((total.shape[0] - latent, inner), F32)
            place_blocks(
                total, latent // devices, place, turn, range(devices // 2), [target + (0, 0, rows_k)]
            )
            if target is of_v or not shared:
                write(2 * target[0])
        targets = [of_r + (shared, 0, rows_q - shared)]
        if shared:
            targets.append(of_p + (0, rows_k, shared))
        tile = total_q.shape[1]
        pltpu.make_async_copy(normed_hbm, normed_t, normed_sem).wait()
        for at in range(0, normed_t.shape[0], tile):
            part = total_q.at[at // tile % 2]
            part[...] = dot(normed_t[at : at + tile, :], query_grad[...], nn)
            pairs = range(at // rows_q // 2, (at + tile) // rows_q // 2)
            place_blocks(part, rows_q, place, turn, pairs, targets)
        if shared:
            write(2)
        write(4)
        for n in range(6):
            pltpu.make_async_copy(staged[n], results[n], out_sem.at[n]).wait()


def held(value, after):
    return pl.pallas_call(
        lambda *refs: None,
        out_shape=jax.ShapeDtypeStruct(value.shape, value.dtype),
        in_specs=[ANY] * (1 + len(after)),
        out_specs=ANY,
        input_output_aliases={0: 0},
    )(value, *after)


def swap(value, bit, devices):
    return lax.ppermute(value, AXES, [(i, i ^ bit) for i in range(devices)])


def body(tokens, ctx_cotangent, latent_cache, nbr_ids, w_query, w_key, w_value):
    owners, shards = lax.axis_size("dp"), lax.axis_size("shard")
    devices = owners * shards
    owned, slice_tokens, latent = latent_cache.shape
    spans, nbr = nbr_ids.shape
    each = spans * nbr
    group = each * shards
    slots = 2 * group // owners
    inner = w_query.shape[1]
    heads = inner // HEAD_DIM
    scale = HEAD_DIM**-0.5
    span = tokens.shape[0] // spans
    dp, shard = lax.axis_index("dp"), lax.axis_index("shard")
    place = jnp.stack([dp, shard, dp * shards + shard]).astype(jnp.int32)

    ids = lax.all_to_all(
        jnp.broadcast_to(nbr_ids.reshape(1, each), (devices, each)),
        AXES,
        split_axis=0,
        concat_axis=0,
        tiled=True,
    )
    as_float = tokens.astype(F32)
    normed = (
        as_float
        * lax.rsqrt(jnp.mean(as_float * as_float, axis=-1, keepdims=True) + 1e-06)
    ).astype(BF16)

    heights = [w.shape[0] for w in (w_query, w_key, w_value)]

    def serve(start, width, by_peer, lay=(), after=()):
        lengths = [slots] * owners if by_peer else [owners * slots]
        shapes = [
            jax.ShapeDtypeStruct((n, slice_tokens, width), BF16) for n in lengths
        ]
        if lay:
            shapes.append(jax.ShapeDtypeStruct((sum(heights), inner), BF16))
        return pl.pallas_call(
            functools.partial(
                serve_kernel, owners, slots, owned, start, len(lay), len(after)
            ),
            out_shape=shapes,
            in_specs=[SMEM, SMEM, HBM] + [HBM] * len(lay) + [ANY] * len(after),
            out_specs=[VMEM] * len(shapes),
            scratch_shapes=[
                pltpu.SMEM((owners * slots + 1,), jnp.int32),
                pltpu.SemaphoreType.DMA,
            ],
            compiler_params=pltpu.CompilerParams(vmem_limit_bytes=58 << 20),
        )(ids, place, latent_cache, *lay, *after)

    def send(rows):
        return lax.all_to_all(rows, "dp", split_axis=0, concat_axis=0, tiled=True)

    def pick(arrived, width, after=()):
        picked = pl.pallas_call(
            functools.partial(
                pick_kernel, owners, slots, shards, owned, len(arrived), len(after)
            ),
            out_shape=[jax.ShapeDtypeStruct((each, slice_tokens, width), BF16)]
            * shards,
            in_specs=[SMEM, SMEM] + [ANY] * (len(arrived) + len(after)),
            out_specs=[VMEM] * shards,
            scratch_shapes=[
                pltpu.SMEM((owners + group,), jnp.int32),
                pltpu.SemaphoreType.DMA,
            ],
            compiler_params=pltpu.CompilerParams(vmem_limit_bytes=16 << 20),
        )(ids, place, *arrived, *after)
        return [
            piece if k == 0 else swap(piece, k, devices)
            for k, piece in enumerate(picked)
        ]

    cut_0, cut_1, cut_2 = lane_cuts(latent, (3, 3, 1))
    rows_0, weights = serve(*cut_0, False, (w_query, w_key, w_value))
    arrived_0 = send(rows_0)
    weights = lax.all_gather(weights, "shard", axis=0)
    rows_1 = serve(*cut_1, True, (), [rows_0])
    arrived_1 = [
        part if k == 0 else swap(part, k * shards, devices)
        for k, part in enumerate(rows_1)
    ]
    pieces_0 = pick([arrived_0], cut_0[1])
    query_full = weights[:, : heights[0]].reshape(-1, inner)
    query_sum = jnp.dot(normed, query_full, preferred_element_type=F32)
    queries = (query_sum * scale).astype(BF16)
    normed_t = normed.T
    (rows_2,) = serve(*cut_2, False, (), [rows_1[0]])
    rows_2 = held(rows_2, [arrived_0, *arrived_1[1:], queries, pieces_0[0]])
    arrived_2 = send(rows_2)
    pieces_1 = pick(arrived_1, cut_1[1])
    pieces_2 = pick([arrived_2], cut_2[1], pieces_1[:1])
    pieces = pieces_0 + pieces_1 + pieces_2

    keys = nbr * shards * slice_tokens
    width_q = tokens.shape[1]
    by_span = pl.BlockSpec((span, inner), lambda c: (c, 0))

    low = 1 << (owners.bit_length() - 1) // 2
    length = dict(z=owners // low, x=low, y=shards // 2)
    bit = dict(z=low * shards, x=shards, y=2)
    orders = ("zyx", "yxz", "xyz")

    def turn(rel, which):
        at = dict(
            y=rel % length["y"],
            x=rel // length["y"] % length["x"],
            z=rel // (length["y"] * length["x"]),
        )
        first, second, third = orders[which]
        return (at[first] * length[second] + at[second]) * length[third] + at[third]

    rows_k = -(-latent // devices // 16) * 16
    rows_q = width_q // devices
    shared = rows_q // 64 * 16
    blocks = []
    for rows in (rows_k, rows_k + shared, rows_q - shared):
        shape = (devices // 2, rows, inner)
        blocks += [jax.ShapeDtypeStruct(shape, BF16)] * 2
    spare = rows_k
    context, *blocks = pl.pallas_call(
        functools.partial(
            attend_kernel,
            len(pieces) // shards,
            shards,
            heads,
            scale,
            devices,
            spans,
            turn,
        ),
        grid=(spans,),
        out_shape=[jax.ShapeDtypeStruct((spans * span, inner), BF16)] + blocks,
        in_specs=[
            pl.BlockSpec((nbr, slice_tokens, piece.shape[2]), lambda c: (c, 0, 0))
            for piece in pieces
        ]
        + [SMEM, by_span, by_span, ANY, ANY],
        out_specs=[by_span] + [ANY] * len(blocks),
        scratch_shapes=[pltpu.VMEM((keys, inner), BF16)] * 2
        + [pltpu.VMEM((heads * span, keys), F32)] * 2
        + [pltpu.VMEM((heads * span, keys), BF16)] * 2
        + [
            pltpu.VMEM((spans, latent, keys), BF16),
            pltpu.VMEM((spans * span, inner), BF16),
        ]
        + [pltpu.VMEM((spans * keys, inner), BF16)] * 2
        + [pltpu.VMEM((latent + spare, inner), F32)] * 2
        + [pltpu.VMEM((2, 8 * width_q // devices, inner), F32)]
        + [pltpu.VMEM(block.shape, BF16) for block in blocks]
        + [pltpu.VMEM((latent, inner), BF16)] * 2
        + [
            pltpu.VMEM(normed_t.shape, BF16),
            pltpu.SemaphoreType.DMA((2,)),
            pltpu.SemaphoreType.DMA,
            pltpu.SemaphoreType.DMA((6,)),
        ],
        compiler_params=pltpu.CompilerParams(vmem_limit_bytes=58 << 20),
        cost_estimate=pl.CostEstimate(
            flops=2 * inner * (4 * spans * keys * (latent + 2 * span) + tokens.size),
            bytes_accessed=12 * (2 * latent + width_q) * inner,
            transcendentals=spans * span * keys * heads,
        ),
    )(*pieces, place, queries, ctx_cotangent, normed_t, weights)

    def travel(sends, axis):
        return [swap(part, k * bit[axis], devices) for k, part in enumerate(sends, 1)]

    keep_v, send_v, keep_p, send_p, keep_r, send_r = blocks
    came_r, came_p, came_v = (swap(s, 1, devices) for s in (send_r, send_p, send_v))
    keep_r, sends = combine([[keep_r, came_r]], length["x"])
    came_r = travel(sends, "x")
    keep_p, sends = combine([[keep_p, came_p]], length["y"], sends[:1])
    came_p = travel(sends, "y")
    keep_v, sends = combine([[keep_v, came_v]], length["z"], sends[:1])
    came_v = travel(sends, "z")
    keep_p, sends = combine([[keep_p, *came_p]], length["x"], came_v[:1])
    came_p = travel(sends, "x")
    keep_r, sends = combine([[keep_r, *came_r]], length["y"], [*sends[:1], *came_v[:2]])
    came_r = travel(sends, "y")
    keep_v, sends = combine([[keep_v, *came_v]], length["y"], sends[:1])
    came_v = travel(sends, "y")
    keep, sends = combine(
        [[keep_p, *came_p], [keep_r, *came_r]], length["z"], sends[:1]
    )
    came = travel(sends, "z")
    keep_v, sends = combine([[keep_v, *came_v]], length["x"], sends[:1])
    came_v = travel(sends, "x")
    ends = [keep_v, *came_v, keep, *came]
    grad_query, grad_key, grad_value = pl.pallas_call(
        functools.partial(finish_kernel, 1 + len(came_v), rows_k),
        out_shape=[
            jax.ShapeDtypeStruct((rows_q, inner), F32),
            jax.ShapeDtypeStruct((latent // devices, inner), F32),
            jax.ShapeDtypeStruct((latent // devices, inner), F32),
        ],
        in_specs=[VMEM] * len(ends),
        out_specs=[VMEM] * 3,
        compiler_params=pltpu.CompilerParams(vmem_limit_bytes=16 << 20),
    )(*ends)
    return context, grad_query, grad_key, grad_value


def solution(mesh):
    rows = P(AXES, None)
    by_shard = P("shard", None)
    return jax.shard_map(
        body,
        mesh=mesh,
        in_specs=(rows, rows, P("dp", "shard", None), rows)
        + (by_shard, by_shard, by_shard),
        out_specs=(rows, rows, rows, rows),
        check_vma=False,
    )
```

```python
import functools

import jax
import jax.numpy as jnp
from jax import lax
from jax.experimental import pallas as pl
from jax.experimental.pallas import tpu as pltpu
from jax.sharding import PartitionSpec as P

HEAD_DIM = 128
AXES = ("dp", "shard")
LANES = 128
ANY = pl.BlockSpec(memory_space=pl.ANY)
HBM = pl.BlockSpec(memory_space=pltpu.HBM)
SMEM = pl.BlockSpec(memory_space=pltpu.SMEM)
VMEM = pl.BlockSpec(memory_space=pltpu.VMEM)
F32 = jnp.float32
BF16 = jnp.bfloat16


def lane_cuts(width, shares):
    tiles = width // LANES
    total = sum(shares)
    ends = [0]
    for k in range(1, len(shares) + 1):
        ends.append(round(tiles * sum(shares[:k]) / total) * LANES)
    return [(a, b - a) for a, b in zip(ends, ends[1:]) if b > a]


def serve_kernel(owners, slots, owned, start, lay, after, ids, place, cache, *rest):
    parts, (*outs, table, sem) = rest[:lay], rest[lay + after :]
    if lay:
        *outs, joined = outs
        at = 0
        for part in parts:
            size = part.shape[0]
            pltpu.make_async_copy(part, joined.at[pl.ds(at, size)], sem).start()
            at += size
    me = place[0]
    shards, each = ids.shape[0] // owners, ids.shape[1]
    width = outs[0].shape[2]
    for k in range(owners):
        asking = jnp.bitwise_xor(me, k)
        base = k * slots

        def scan(s, at):
            for i in range(each):
                row = ids[asking * shards + s, i] - me * owned
                mine = jnp.logical_and(row >= 0, row < owned)
                table[at] = jnp.clip(row, 0, owned - 1)
                at = jnp.where(mine, at + 1, at)
            return at

        at = lax.fori_loop(0, shards, scan, base)
        for j in range(slots):
            row = jnp.where(base + j < at, table[base + j], 0)
            into = outs[0].at[asking * slots + j] if len(outs) == 1 else outs[k].at[j]
            pltpu.make_async_copy(
                cache.at[row, :, pl.ds(start, width)], into, sem
            ).start()
    for out in outs + [joined] if lay else outs:
        pltpu.make_async_copy(out, out, sem).wait()


def pick_kernel(owners, slots, shards, owned, lanes, after, ids, place, *rest):
    arrived, rest = rest[:lanes], rest[lanes + after :]
    outs = rest[:shards]
    count, sem = rest[shards:]
    me, shard = place[0], place[1]
    each = ids.shape[1]
    for k in range(owners):
        count[k] = 0

    def locate(s, carry):
        for i in range(each):
            owner = ids[me * shards + s, i] // owned
            at = count[owner]
            count[owner] = at + 1
            count[owners + s * each + i] = at
        return carry

    lax.fori_loop(0, shards, locate, 0)
    for k in range(shards):
        peer = jnp.bitwise_xor(shard, k)
        for j in range(each):
            owner = ids[me * shards + peer, j] // owned
            at = count[owners + peer * each + j]
            if lanes == 1:
                pltpu.make_async_copy(
                    arrived[0].at[owner * slots + at], outs[k].at[j], sem
                ).start()
                continue
            for n in range(owners):

                @pl.when(jnp.bitwise_xor(owner, me) == n)
                def _(n=n, k=k, j=j, at=at):
                    pltpu.make_async_copy(
                        arrived[n].at[at], outs[k].at[j], sem
                    ).start()

    for out in outs:
        pltpu.make_async_copy(out, out, sem).wait()


def place_blocks(total, rows, place, turn, pairs, targets):
    me = place[2]
    odd = jnp.bitwise_and(me, 1) == 1
    half = me >> 1
    for d in pairs:
        rel = jnp.bitwise_xor(half, d)
        for order, keep, send, source, into, size in targets:
            even_at = 2 * (d - pairs[0]) * rows + source
            odd_at = even_at + rows
            even_rows = total[even_at : even_at + size, :]
            odd_rows = total[odd_at : odd_at + size, :]
            at = turn(rel, order)
            keep[at, into : into + size, :] = jnp.where(odd, odd_rows, even_rows).astype(
                BF16
            )
            send[at, into : into + size, :] = jnp.where(odd, even_rows, odd_rows).astype(
                BF16
            )


def combine_kernel(counts, split, after, *refs):
    inputs, outs = [], refs[sum(counts) + after :]
    for count in counts:
        inputs.append(refs[:count])
        refs = refs[count:]
    each = inputs[0][0].shape[0] // split
    for k in range(split):
        at = 0
        for parts in inputs:
            rows = parts[0].shape[1]

            def one(i, carry, k=k, at=at, rows=rows, parts=parts):
                total = parts[0][k * each + i].astype(F32)
                for part in parts[1:]:
                    total = total + part[k * each + i].astype(F32)
                outs[k][i, at : at + rows, :] = total.astype(outs[k].dtype)
                return carry

            lax.fori_loop(0, each, one, 0)
            at += rows


def finish_kernel(first, rows_k, *refs):
    ends, (grad_query, grad_key, grad_value) = refs[:-3], refs[-3:]

    def total(parts, at, size):
        result = parts[0][0, at : at + size, :]
        for part in parts[1:]:
            result = result + part[0, at : at + size, :].astype(F32)
        return result

    exact = grad_key.shape[0]
    grad_value[...] = total(ends[:first], 0, rows_k)[:exact]
    grad_key[...] = total(ends[first:], 0, rows_k)[:exact]
    grad_query[...] = total(ends[first:], rows_k, grad_query.shape[0])


def combine(groups, split, after=()):
    lead, _, columns = groups[0][0].shape
    rows = sum(group[0].shape[1] for group in groups)
    shape = (lead // split, rows, columns)
    flat = [array for group in groups for array in group]
    body = functools.partial(
        combine_kernel, [len(group) for group in groups], split, len(after)
    )
    moved = sum(array.size * array.dtype.itemsize for array in flat)
    keep, *sends = pl.pallas_call(
        body,
        out_shape=[jax.ShapeDtypeStruct(shape, F32)]
        + [jax.ShapeDtypeStruct(shape, BF16)] * (split - 1),
        in_specs=[VMEM] * len(flat) + [ANY] * len(after),
        out_specs=[VMEM] * split,
        compiler_params=pltpu.CompilerParams(vmem_limit_bytes=2 * moved + (4 << 20)),
    )(*flat, *after)
    return keep, sends


def attend_kernel(parts, shards, heads, scale, devices, spans, turn, *refs):
    pieces, refs = refs[: parts * shards], refs[parts * shards :]
    place, queries_hbm, cotangent_hbm, normed_hbm, weights = refs[:5]
    context, keep_v, send_v, keep_p, send_p, keep_r, send_r = refs[5:12]
    refs = refs[12:]
    key_rows, value_rows, scores, prob_grads, prob_rounds, score_grads = refs[:6]
    latents_t, query_grad, key_grad, value_grad, total_v, total_k, total_q = refs[6:13]
    w_key, w_value, normed_t, all_queries, all_cotangent = refs[13:18]
    held_pieces, sems = refs[18 : 18 + parts], refs[18 + parts]
    step = pl.program_id(0)
    _, nbr, tokens, _ = held_pieces[0].shape
    nbr = nbr // spans
    of_step = pl.ds(step * nbr, nbr)
    span = all_queries.shape[0] // spans
    of_span = pl.ds(pl.multiple_of(step * span, span), span)
    queries, cotangent = all_queries.at[of_span], all_cotangent.at[of_span]
    each = w_key.shape[0] // shards
    skipped = weights.shape[1] - 2 * each

    @pl.when(step == 0)
    def _():
        for j in range(parts):
            for k in range(shards):
                pltpu.make_async_copy(
                    pieces[j * shards + k], held_pieces[j].at[k], sems.at[0]
                ).start()
        for which, held_weights in enumerate((w_key, w_value)):
            for k in range(shards):
                pltpu.make_async_copy(
                    weights.at[k, pl.ds(skipped + which * each, each)],
                    held_weights.at[pl.ds(k * each, each)],
                    sems.at[1 + which],
                ).start()
        pltpu.make_async_copy(queries_hbm, all_queries, sems.at[3]).start()
        pltpu.make_async_copy(cotangent_hbm, all_cotangent, sems.at[4]).start()
        pltpu.make_async_copy(normed_hbm, normed_t, sems.at[5]).start()
        for ref in held_pieces:
            pltpu.make_async_copy(ref, ref, sems.at[0]).wait()
        pltpu.make_async_copy(w_key, w_key, sems.at[1]).wait()
        pltpu.make_async_copy(w_value, w_value, sems.at[2]).wait()
        pltpu.make_async_copy(queries_hbm, all_queries, sems.at[3]).wait()
        pltpu.make_async_copy(cotangent_hbm, all_cotangent, sems.at[4]).wait()

    rows = jnp.concatenate(
        [
            jnp.concatenate(
                [
                    held_pieces[j][k, of_step].reshape(nbr * tokens, -1)
                    for j in range(parts)
                ],
                axis=1,
            )
            for k in range(shards)
        ],
        axis=0,
    )
    keys, latent = rows.shape
    inner = queries.shape[1]
    latents_t[step] = rows.T
    key_rows[...] = jnp.dot(rows, w_key[...], preferred_element_type=F32).astype(BF16)
    value_rows[...] = jnp.dot(rows, w_value[...], preferred_element_type=F32).astype(
        BF16
    )
    dot = functools.partial(lax.dot_general, preferred_element_type=F32)
    nt = (((1,), (1,)), ((), ()))
    nn = (((1,), (0,)), ((), ()))
    tn = (((0,), (0,)), ((), ()))
    of_keys = pl.ds(pl.multiple_of(step * keys, keys), keys)

    def at_head(h):
        return slice(h * span, (h + 1) * span), slice(h * HEAD_DIM, (h + 1) * HEAD_DIM)

    for h in range(heads):
        stacked, cols = at_head(h)
        scores[stacked, :] = dot(queries[:, cols], key_rows[:, cols], nt)
        prob_grads[stacked, :] = dot(cotangent[:, cols], value_rows[:, cols], nt)
    for h in range(heads):
        stacked, _ = at_head(h)
        score = scores[stacked, :]
        raised = jnp.exp(score - jnp.max(score, axis=-1, keepdims=True))
        prob = raised * (1.0 / jnp.sum(raised, axis=-1, keepdims=True))
        prob_rounds[stacked, :] = prob.astype(BF16)
        prob_grad = prob_grads[stacked, :]
        inner_sum = jnp.sum(prob * prob_grad, axis=-1, keepdims=True)
        score_grads[stacked, :] = (prob * (prob_grad - inner_sum)).astype(BF16)
    for h in range(heads):
        stacked, cols = at_head(h)
        prob, score_grad = prob_rounds[stacked, :], score_grads[stacked, :]
        context[:, cols] = dot(prob, value_rows[:, cols], nn).astype(BF16)
        value_grad[of_keys, cols] = dot(prob, cotangent[:, cols], tn).astype(BF16)
        query_grad[of_span, cols] = (
            dot(score_grad, key_rows[:, cols], nn) * scale
        ).astype(BF16)
        key_grad[of_keys, cols] = dot(score_grad, queries[:, cols], tn).astype(BF16)

    @pl.when(step == spans - 1)
    def _():
        across = jnp.concatenate([latents_t[c] for c in range(spans)], axis=1)
        of_v, of_p, of_r = (0, keep_v, send_v), (1, keep_p, send_p), (2, keep_r, send_r)
        rows_k, rows_q = keep_v.shape[1], normed_t.shape[0] // devices
        shared = keep_p.shape[1] - rows_k
        for total, grad, target in ((total_v, value_grad, of_v), (total_k, key_grad, of_p)):
            total[:latent, :] = dot(across, grad[...], nn)
            total[latent:, :] = jnp.zeros((total.shape[0] - latent, inner), F32)
            place_blocks(
                total, latent // devices, place, turn, range(devices // 2), [target + (0, 0, rows_k)]
            )
        targets = [of_r + (shared, 0, rows_q - shared)]
        if shared:
            targets.append(of_p + (0, rows_k, shared))
        tile = total_q.shape[1]
        pltpu.make_async_copy(normed_hbm, normed_t, sems.at[5]).wait()
        for at in range(0, normed_t.shape[0], tile):
            part = total_q.at[at // tile % 2]
            part[...] = dot(normed_t[at : at + tile, :], query_grad[...], nn)
            pairs = range(at // rows_q // 2, (at + tile) // rows_q // 2)
            place_blocks(part, rows_q, place, turn, pairs, targets)


def swap(value, bit, devices):
    return lax.ppermute(value, AXES, [(i, i ^ bit) for i in range(devices)])


def body(tokens, ctx_cotangent, latent_cache, nbr_ids, w_query, w_key, w_value):
    owners, shards = lax.axis_size("dp"), lax.axis_size("shard")
    devices = owners * shards
    owned, slice_tokens, latent = latent_cache.shape
    spans, nbr = nbr_ids.shape
    each = spans * nbr
    group = each * shards
    slots = 2 * group // owners
    inner = w_query.shape[1]
    heads = inner // HEAD_DIM
    scale = HEAD_DIM**-0.5
    span = tokens.shape[0] // spans
    dp, shard = lax.axis_index("dp"), lax.axis_index("shard")
    place = jnp.stack([dp, shard, dp * shards + shard]).astype(jnp.int32)

    ids = lax.all_to_all(
        jnp.broadcast_to(nbr_ids.reshape(1, each), (devices, each)),
        AXES,
        split_axis=0,
        concat_axis=0,
        tiled=True,
    )
    as_float = tokens.astype(F32)
    normed = (
        as_float
        * lax.rsqrt(jnp.mean(as_float * as_float, axis=-1, keepdims=True) + 1e-06)
    ).astype(BF16)

    heights = [w.shape[0] for w in (w_query, w_key, w_value)]

    def serve(start, width, by_peer, lay=(), after=()):
        lengths = [slots] * owners if by_peer else [owners * slots]
        shapes = [
            jax.ShapeDtypeStruct((n, slice_tokens, width), BF16) for n in lengths
        ]
        if lay:
            shapes.append(jax.ShapeDtypeStruct((sum(heights), inner), BF16))
        return pl.pallas_call(
            functools.partial(
                serve_kernel, owners, slots, owned, start, len(lay), len(after)
            ),
            out_shape=shapes,
            in_specs=[SMEM, SMEM, HBM] + [HBM] * len(lay) + [ANY] * len(after),
            out_specs=[VMEM] * len(shapes),
            scratch_shapes=[
                pltpu.SMEM((owners * slots + 1,), jnp.int32),
                pltpu.SemaphoreType.DMA,
            ],
            compiler_params=pltpu.CompilerParams(vmem_limit_bytes=58 << 20),
        )(ids, place, latent_cache, *lay, *after)

    def pick(arrived, width, after=()):
        picked = pl.pallas_call(
            functools.partial(
                pick_kernel, owners, slots, shards, owned, len(arrived), len(after)
            ),
            out_shape=[jax.ShapeDtypeStruct((each, slice_tokens, width), BF16)]
            * shards,
            in_specs=[SMEM, SMEM] + [ANY] * (len(arrived) + len(after)),
            out_specs=[VMEM] * shards,
            scratch_shapes=[
                pltpu.SMEM((owners + group,), jnp.int32),
                pltpu.SemaphoreType.DMA,
            ],
            compiler_params=pltpu.CompilerParams(vmem_limit_bytes=16 << 20),
        )(ids, place, *arrived, *after)
        return [
            piece if k == 0 else swap(piece, k, devices)
            for k, piece in enumerate(picked)
        ]

    cut_0, cut_1 = lane_cuts(latent, (4, 3))
    rows_0, weights = serve(*cut_0, False, (w_query, w_key, w_value))
    arrived_0 = lax.all_to_all(rows_0, "dp", split_axis=0, concat_axis=0, tiled=True)
    weights = lax.all_gather(weights, "shard", axis=0)
    rows_1 = serve(*cut_1, True, (), [rows_0])
    arrived_1 = [
        part if k == 0 else swap(part, k * shards, devices)
        for k, part in enumerate(rows_1)
    ]
    pieces_0 = pick([arrived_0], cut_0[1])
    query_full = weights[:, : heights[0]].reshape(-1, inner)
    query_sum = jnp.dot(normed, query_full, preferred_element_type=F32)
    queries = (query_sum * scale).astype(BF16)
    normed_t = normed.T
    pieces_1 = pick(arrived_1, cut_1[1], [queries, normed_t, pieces_0[0]])
    pieces = pieces_0 + pieces_1

    keys = nbr * shards * slice_tokens
    width_q = tokens.shape[1]
    by_span = pl.BlockSpec((span, inner), lambda c: (c, 0))

    low = 1 << (owners.bit_length() - 1) // 2
    length = dict(z=owners // low, x=low, y=shards // 2)
    bit = dict(z=low * shards, x=shards, y=2)
    orders = ("zyx", "yxz", "xyz")

    def turn(rel, which):
        at = dict(
            y=rel % length["y"],
            x=rel // length["y"] % length["x"],
            z=rel // (length["y"] * length["x"]),
        )
        first, second, third = orders[which]
        return (at[first] * length[second] + at[second]) * length[third] + at[third]

    rows_k = -(-latent // devices // 16) * 16
    rows_q = width_q // devices
    shared = rows_q // 64 * 16
    blocks = []
    for rows in (rows_k, rows_k + shared, rows_q - shared):
        shape = (devices // 2, rows, inner)
        blocks += [jax.ShapeDtypeStruct(shape, BF16)] * 2
    spare = rows_k
    context, *blocks = pl.pallas_call(
        functools.partial(
            attend_kernel,
            len(pieces) // shards,
            shards,
            heads,
            scale,
            devices,
            spans,
            turn,
        ),
        grid=(spans,),
        out_shape=[jax.ShapeDtypeStruct((spans * span, inner), BF16)] + blocks,
        in_specs=[HBM] * len(pieces) + [SMEM] + [HBM] * 4,
        out_specs=[by_span] + [VMEM] * len(blocks),
        scratch_shapes=[pltpu.VMEM((keys, inner), BF16)] * 2
        + [pltpu.VMEM((heads * span, keys), F32)] * 2
        + [pltpu.VMEM((heads * span, keys), BF16)] * 2
        + [
            pltpu.VMEM((spans, latent, keys), BF16),
            pltpu.VMEM((spans * span, inner), BF16),
        ]
        + [pltpu.VMEM((spans * keys, inner), BF16)] * 2
        + [pltpu.VMEM((latent + spare, inner), F32)] * 2
        + [pltpu.VMEM((2, 8 * width_q // devices, inner), F32)]
        + [pltpu.VMEM((latent, inner), BF16)] * 2
        + [pltpu.VMEM(normed_t.shape, BF16)]
        + [pltpu.VMEM(queries.shape, BF16)] * 2
        + [
            pltpu.VMEM((shards, *piece.shape), BF16)
            for piece in pieces[:: shards]
        ]
        + [pltpu.SemaphoreType.DMA((6,))],
        compiler_params=pltpu.CompilerParams(vmem_limit_bytes=40 << 20),
        cost_estimate=pl.CostEstimate(
            flops=2 * inner * (4 * spans * keys * (latent + 2 * span) + tokens.size),
            bytes_accessed=12 * (2 * latent + width_q) * inner,
            transcendentals=spans * span * keys * heads,
        ),
    )(*pieces, place, queries, ctx_cotangent, normed_t, weights)

    def travel(sends, axis):
        return [swap(part, k * bit[axis], devices) for k, part in enumerate(sends, 1)]

    keep_v, send_v, keep_p, send_p, keep_r, send_r = blocks
    came_r, came_p, came_v = (swap(s, 1, devices) for s in (send_r, send_p, send_v))
    keep_r, sends = combine([[keep_r, came_r]], length["x"])
    came_r = travel(sends, "x")
    keep_p, sends = combine([[keep_p, came_p]], length["y"], sends[:1])
    came_p = travel(sends, "y")
    keep_v, sends = combine([[keep_v, came_v]], length["z"], sends[:1])
    came_v = travel(sends, "z")
    keep_p, sends = combine([[keep_p, *came_p]], length["x"], came_v[:1])
    came_p = travel(sends, "x")
    keep_r, sends = combine([[keep_r, *came_r]], length["y"], [*sends[:1], *came_v[:2]])
    came_r = travel(sends, "y")
    keep_v, sends = combine([[keep_v, *came_v]], length["y"], sends[:1])
    came_v = travel(sends, "y")
    keep, sends = combine(
        [[keep_p, *came_p], [keep_r, *came_r]], length["z"], sends[:1]
    )
    came = travel(sends, "z")
    keep_v, sends = combine([[keep_v, *came_v]], length["x"], sends[:1])
    came_v = travel(sends, "x")
    ends = [keep_v, *came_v, keep, *came]
    grad_query, grad_key, grad_value = pl.pallas_call(
        functools.partial(finish_kernel, 1 + len(came_v), rows_k),
        out_shape=[
            jax.ShapeDtypeStruct((rows_q, inner), F32),
            jax.ShapeDtypeStruct((latent // devices, inner), F32),
            jax.ShapeDtypeStruct((latent // devices, inner), F32),
        ],
        in_specs=[VMEM] * len(ends),
        out_specs=[VMEM] * 3,
        compiler_params=pltpu.CompilerParams(vmem_limit_bytes=16 << 20),
    )(*ends)
    return context, grad_query, grad_key, grad_value


def solution(mesh):
    rows = P(AXES, None)
    by_shard = P("shard", None)
    return jax.shard_map(
        body,
        mesh=mesh,
        in_specs=(rows, rows, P("dp", "shard", None), rows)
        + (by_shard, by_shard, by_shard),
        out_specs=(rows, rows, rows, rows),
        check_vma=False,
    )
```

```python
import functools

import jax
import jax.numpy as jnp
from jax import lax
from jax.experimental import pallas as pl
from jax.experimental.pallas import tpu as pltpu
from jax.sharding import PartitionSpec as P

HEAD_DIM = 128
AXES = ("dp", "shard")
LANES = 128
ANY = pl.BlockSpec(memory_space=pl.ANY)
HBM = pl.BlockSpec(memory_space=pltpu.HBM)
SMEM = pl.BlockSpec(memory_space=pltpu.SMEM)
VMEM = pl.BlockSpec(memory_space=pltpu.VMEM)
F32 = jnp.float32
BF16 = jnp.bfloat16


def lane_cuts(width, shares):
    tiles = width // LANES
    total = sum(shares)
    ends = [0]
    for k in range(1, len(shares) + 1):
        ends.append(round(tiles * sum(shares[:k]) / total) * LANES)
    return [(a, b - a) for a, b in zip(ends, ends[1:]) if b > a]


def serve_kernel(owners, slots, owned, start, lay, after, ids, place, cache, *rest):
    parts, (*outs, table, sem) = rest[:lay], rest[lay + after :]
    if lay:
        *outs, joined = outs
        at = 0
        for part in parts:
            size = part.shape[0]
            pltpu.make_async_copy(part, joined.at[pl.ds(at, size)], sem).start()
            at += size
    me = place[0]
    shards, each = ids.shape[0] // owners, ids.shape[1]
    width = outs[0].shape[2]
    for k in range(owners):
        asking = jnp.bitwise_xor(me, k)
        base = k * slots

        def scan(s, at):
            for i in range(each):
                row = ids[asking * shards + s, i] - me * owned
                mine = jnp.logical_and(row >= 0, row < owned)
                table[at] = jnp.clip(row, 0, owned - 1)
                at = jnp.where(mine, at + 1, at)
            return at

        at = lax.fori_loop(0, shards, scan, base)
        for j in range(slots):
            row = jnp.where(base + j < at, table[base + j], 0)
            into = outs[0].at[asking * slots + j] if len(outs) == 1 else outs[k].at[j]
            pltpu.make_async_copy(
                cache.at[row, :, pl.ds(start, width)], into, sem
            ).start()
    for out in outs + [joined] if lay else outs:
        pltpu.make_async_copy(out, out, sem).wait()


def pick_kernel(owners, slots, shards, owned, lanes, after, ids, place, *rest):
    arrived, rest = rest[:lanes], rest[lanes + after :]
    outs = rest[:shards]
    count, sem = rest[shards:]
    me, shard = place[0], place[1]
    each = ids.shape[1]
    for k in range(owners):
        count[k] = 0

    def locate(s, carry):
        for i in range(each):
            owner = ids[me * shards + s, i] // owned
            at = count[owner]
            count[owner] = at + 1
            count[owners + s * each + i] = at
        return carry

    lax.fori_loop(0, shards, locate, 0)
    for k in range(shards):
        peer = jnp.bitwise_xor(shard, k)
        for j in range(each):
            owner = ids[me * shards + peer, j] // owned
            at = count[owners + peer * each + j]
            if lanes == 1:
                pltpu.make_async_copy(
                    arrived[0].at[owner * slots + at], outs[k].at[j], sem
                ).start()
                continue
            for n in range(owners):

                @pl.when(jnp.bitwise_xor(owner, me) == n)
                def _(n=n, k=k, j=j, at=at):
                    pltpu.make_async_copy(
                        arrived[n].at[at], outs[k].at[j], sem
                    ).start()

    for out in outs:
        pltpu.make_async_copy(out, out, sem).wait()


def project_kernel(scale, normed, weights, out, held, sem):
    parts = weights.shape[0]
    rows = held.shape[0] // parts
    for k in range(parts):
        pltpu.make_async_copy(
            weights.at[k, pl.ds(0, rows)], held.at[pl.ds(k * rows, rows)], sem
        ).start()
    pltpu.make_async_copy(held, held, sem).wait()
    total = jnp.dot(normed[...], held[...], preferred_element_type=F32)
    out[...] = (total * scale).astype(BF16)


def place_blocks(total, rows, place, turn, pairs, targets):
    me = place[2]
    odd = jnp.bitwise_and(me, 1) == 1
    half = me >> 1
    for d in pairs:
        rel = jnp.bitwise_xor(half, d)
        for order, keep, send, source, into, size in targets:
            even_at = 2 * (d - pairs[0]) * rows + source
            odd_at = even_at + rows
            even_rows = total[even_at : even_at + size, :]
            odd_rows = total[odd_at : odd_at + size, :]
            at = turn(rel, order)
            keep[at, into : into + size, :] = jnp.where(odd, odd_rows, even_rows).astype(
                BF16
            )
            send[at, into : into + size, :] = jnp.where(odd, even_rows, odd_rows).astype(
                BF16
            )


def combine_kernel(counts, split, after, *refs):
    inputs, outs = [], refs[sum(counts) + after :]
    for count in counts:
        inputs.append(refs[:count])
        refs = refs[count:]
    each = inputs[0][0].shape[0] // split
    for k in range(split):
        at = 0
        for parts in inputs:
            rows = parts[0].shape[1]

            def one(i, carry, k=k, at=at, rows=rows, parts=parts):
                total = parts[0][k * each + i].astype(F32)
                for part in parts[1:]:
                    total = total + part[k * each + i].astype(F32)
                outs[k][i, at : at + rows, :] = total.astype(outs[k].dtype)
                return carry

            lax.fori_loop(0, each, one, 0)
            at += rows


def finish_kernel(first, rows_k, *refs):
    ends, (grad_query, grad_key, grad_value) = refs[:-3], refs[-3:]

    def total(parts, at, size):
        result = parts[0][0, at : at + size, :]
        for part in parts[1:]:
            result = result + part[0, at : at + size, :].astype(F32)
        return result

    exact = grad_key.shape[0]
    grad_value[...] = total(ends[:first], 0, rows_k)[:exact]
    grad_key[...] = total(ends[first:], 0, rows_k)[:exact]
    grad_query[...] = total(ends[first:], rows_k, grad_query.shape[0])


def combine(groups, split, after=()):
    lead, _, columns = groups[0][0].shape
    rows = sum(group[0].shape[1] for group in groups)
    shape = (lead // split, rows, columns)
    flat = [array for group in groups for array in group]
    body = functools.partial(
        combine_kernel, [len(group) for group in groups], split, len(after)
    )
    moved = sum(array.size * array.dtype.itemsize for array in flat)
    keep, *sends = pl.pallas_call(
        body,
        out_shape=[jax.ShapeDtypeStruct(shape, F32)]
        + [jax.ShapeDtypeStruct(shape, BF16)] * (split - 1),
        in_specs=[VMEM] * len(flat) + [ANY] * len(after),
        out_specs=[VMEM] * split,
        compiler_params=pltpu.CompilerParams(vmem_limit_bytes=2 * moved + (4 << 20)),
    )(*flat, *after)
    return keep, sends


def attend_kernel(parts, shards, heads, scale, devices, spans, turn, *refs):
    pieces, refs = refs[: parts * shards], refs[parts * shards :]
    place, queries_hbm, cotangent_hbm, normed_hbm, weights = refs[:5]
    context, keep_v, send_v, keep_p, send_p, keep_r, send_r = refs[5:12]
    refs = refs[12:]
    key_rows, value_rows, scores, prob_grads, prob_rounds, score_grads = refs[:6]
    latents_t, query_grad, key_grad, value_grad, total_v, total_k, total_q = refs[6:13]
    w_key, w_value, normed_t, all_queries, all_cotangent = refs[13:18]
    held_pieces, sems = refs[18 : 18 + parts], refs[18 + parts]
    step = pl.program_id(0)
    _, nbr, tokens, _ = held_pieces[0].shape
    nbr = nbr // spans
    of_step = pl.ds(step * nbr, nbr)
    span = all_queries.shape[0] // spans
    of_span = pl.ds(pl.multiple_of(step * span, span), span)
    queries, cotangent = all_queries.at[of_span], all_cotangent.at[of_span]
    each = w_key.shape[0] // shards
    skipped = weights.shape[1] - 2 * each

    @pl.when(step == 0)
    def _():
        for j in range(parts):
            for k in range(shards):
                pltpu.make_async_copy(
                    pieces[j * shards + k], held_pieces[j].at[k], sems.at[0]
                ).start()
        for which, held_weights in enumerate((w_key, w_value)):
            for k in range(shards):
                pltpu.make_async_copy(
                    weights.at[k, pl.ds(skipped + which * each, each)],
                    held_weights.at[pl.ds(k * each, each)],
                    sems.at[1 + which],
                ).start()
        pltpu.make_async_copy(queries_hbm, all_queries, sems.at[3]).start()
        pltpu.make_async_copy(cotangent_hbm, all_cotangent, sems.at[4]).start()
        pltpu.make_async_copy(normed_hbm, normed_t, sems.at[5]).start()
        for ref in held_pieces:
            pltpu.make_async_copy(ref, ref, sems.at[0]).wait()
        pltpu.make_async_copy(w_key, w_key, sems.at[1]).wait()
        pltpu.make_async_copy(w_value, w_value, sems.at[2]).wait()
        pltpu.make_async_copy(queries_hbm, all_queries, sems.at[3]).wait()
        pltpu.make_async_copy(cotangent_hbm, all_cotangent, sems.at[4]).wait()

    rows = jnp.concatenate(
        [
            jnp.concatenate(
                [
                    held_pieces[j][k, of_step].reshape(nbr * tokens, -1)
                    for j in range(parts)
                ],
                axis=1,
            )
            for k in range(shards)
        ],
        axis=0,
    )
    keys, latent = rows.shape
    inner = queries.shape[1]
    latents_t[step] = rows.T
    key_rows[...] = jnp.dot(rows, w_key[...], preferred_element_type=F32).astype(BF16)
    value_rows[...] = jnp.dot(rows, w_value[...], preferred_element_type=F32).astype(
        BF16
    )
    dot = functools.partial(lax.dot_general, preferred_element_type=F32)
    nt = (((1,), (1,)), ((), ()))
    nn = (((1,), (0,)), ((), ()))
    tn = (((0,), (0,)), ((), ()))
    of_keys = pl.ds(pl.multiple_of(step * keys, keys), keys)

    def at_head(h):
        return slice(h * span, (h + 1) * span), slice(h * HEAD_DIM, (h + 1) * HEAD_DIM)

    for h in range(heads):
        stacked, cols = at_head(h)
        scores[stacked, :] = dot(queries[:, cols], key_rows[:, cols], nt)
        prob_grads[stacked, :] = dot(cotangent[:, cols], value_rows[:, cols], nt)
    for h in range(heads):
        stacked, _ = at_head(h)
        score = scores[stacked, :]
        raised = jnp.exp(score - jnp.max(score, axis=-1, keepdims=True))
        prob = raised * (1.0 / jnp.sum(raised, axis=-1, keepdims=True))
        prob_rounds[stacked, :] = prob.astype(BF16)
        prob_grad = prob_grads[stacked, :]
        inner_sum = jnp.sum(prob * prob_grad, axis=-1, keepdims=True)
        score_grads[stacked, :] = (prob * (prob_grad - inner_sum)).astype(BF16)
    for h in range(heads):
        stacked, cols = at_head(h)
        prob, score_grad = prob_rounds[stacked, :], score_grads[stacked, :]
        context[:, cols] = dot(prob, value_rows[:, cols], nn).astype(BF16)
        value_grad[of_keys, cols] = dot(prob, cotangent[:, cols], tn).astype(BF16)
        query_grad[of_span, cols] = (
            dot(score_grad, key_rows[:, cols], nn) * scale
        ).astype(BF16)
        key_grad[of_keys, cols] = dot(score_grad, queries[:, cols], tn).astype(BF16)

    @pl.when(step == spans - 1)
    def _():
        across = jnp.concatenate([latents_t[c] for c in range(spans)], axis=1)
        of_v, of_p, of_r = (0, keep_v, send_v), (1, keep_p, send_p), (2, keep_r, send_r)
        rows_k, rows_q = keep_v.shape[1], normed_t.shape[0] // devices
        shared = keep_p.shape[1] - rows_k
        for total, grad, target in ((total_v, value_grad, of_v), (total_k, key_grad, of_p)):
            total[:latent, :] = dot(across, grad[...], nn)
            total[latent:, :] = jnp.zeros((total.shape[0] - latent, inner), F32)
            place_blocks(
                total, latent // devices, place, turn, range(devices // 2), [target + (0, 0, rows_k)]
            )
        targets = [of_r + (shared, 0, rows_q - shared)]
        if shared:
            targets.append(of_p + (0, rows_k, shared))
        tile = total_q.shape[1]
        pltpu.make_async_copy(normed_hbm, normed_t, sems.at[5]).wait()
        for at in range(0, normed_t.shape[0], tile):
            part = total_q.at[at // tile % 2]
            part[...] = dot(normed_t[at : at + tile, :], query_grad[...], nn)
            pairs = range(at // rows_q // 2, (at + tile) // rows_q // 2)
            place_blocks(part, rows_q, place, turn, pairs, targets)


def swap(value, bit, devices):
    return lax.ppermute(value, AXES, [(i, i ^ bit) for i in range(devices)])


def body(tokens, ctx_cotangent, latent_cache, nbr_ids, w_query, w_key, w_value):
    owners, shards = lax.axis_size("dp"), lax.axis_size("shard")
    devices = owners * shards
    owned, slice_tokens, latent = latent_cache.shape
    spans, nbr = nbr_ids.shape
    each = spans * nbr
    group = each * shards
    slots = 2 * group // owners
    inner = w_query.shape[1]
    heads = inner // HEAD_DIM
    scale = HEAD_DIM**-0.5
    span = tokens.shape[0] // spans
    dp, shard = lax.axis_index("dp"), lax.axis_index("shard")
    place = jnp.stack([dp, shard, dp * shards + shard]).astype(jnp.int32)

    ids = lax.all_to_all(
        jnp.broadcast_to(nbr_ids.reshape(1, each), (devices, each)),
        AXES,
        split_axis=0,
        concat_axis=0,
        tiled=True,
    )
    as_float = tokens.astype(F32)
    normed = (
        as_float
        * lax.rsqrt(jnp.mean(as_float * as_float, axis=-1, keepdims=True) + 1e-06)
    ).astype(BF16)

    heights = [w.shape[0] for w in (w_query, w_key, w_value)]

    def serve(start, width, by_peer, lay=(), after=()):
        lengths = [slots] * owners if by_peer else [owners * slots]
        shapes = [
            jax.ShapeDtypeStruct((n, slice_tokens, width), BF16) for n in lengths
        ]
        if lay:
            shapes.append(jax.ShapeDtypeStruct((sum(heights), inner), BF16))
        return pl.pallas_call(
            functools.partial(
                serve_kernel, owners, slots, owned, start, len(lay), len(after)
            ),
            out_shape=shapes,
            in_specs=[SMEM, SMEM, HBM] + [HBM] * len(lay) + [ANY] * len(after),
            out_specs=[VMEM] * len(shapes),
            scratch_shapes=[
                pltpu.SMEM((owners * slots + 1,), jnp.int32),
                pltpu.SemaphoreType.DMA,
            ],
            compiler_params=pltpu.CompilerParams(vmem_limit_bytes=58 << 20),
        )(ids, place, latent_cache, *lay, *after)

    def pick(arrived, width, after=()):
        picked = pl.pallas_call(
            functools.partial(
                pick_kernel, owners, slots, shards, owned, len(arrived), len(after)
            ),
            out_shape=[jax.ShapeDtypeStruct((each, slice_tokens, width), BF16)]
            * shards,
            in_specs=[SMEM, SMEM] + [ANY] * (len(arrived) + len(after)),
            out_specs=[VMEM] * shards,
            scratch_shapes=[
                pltpu.SMEM((owners + group,), jnp.int32),
                pltpu.SemaphoreType.DMA,
            ],
            compiler_params=pltpu.CompilerParams(vmem_limit_bytes=16 << 20),
        )(ids, place, *arrived, *after)
        return [
            piece if k == 0 else swap(piece, k, devices)
            for k, piece in enumerate(picked)
        ]

    cut_0, cut_1 = lane_cuts(latent, (4, 3))
    rows_0, weights = serve(*cut_0, False, (w_query, w_key, w_value))
    arrived_0 = lax.all_to_all(rows_0, "dp", split_axis=0, concat_axis=0, tiled=True)
    weights = lax.all_gather(weights, "shard", axis=0)
    rows_1 = serve(*cut_1, True, (), [rows_0])
    arrived_1 = [
        part if k == 0 else swap(part, k * shards, devices)
        for k, part in enumerate(rows_1)
    ]
    pieces_0 = pick([arrived_0], cut_0[1])
    queries = pl.pallas_call(
        functools.partial(project_kernel, scale),
        out_shape=jax.ShapeDtypeStruct((spans * span, inner), BF16),
        in_specs=[VMEM, HBM],
        out_specs=VMEM,
        scratch_shapes=[
            pltpu.VMEM((tokens.shape[1], inner), BF16),
            pltpu.SemaphoreType.DMA,
        ],
        compiler_params=pltpu.CompilerParams(vmem_limit_bytes=16 << 20),
    )(normed, weights)
    normed_t = normed.T
    pieces_1 = pick(arrived_1, cut_1[1], [queries, normed_t, pieces_0[0]])
    pieces = pieces_0 + pieces_1

    keys = nbr * shards * slice_tokens
    width_q = tokens.shape[1]
    by_span = pl.BlockSpec((span, inner), lambda c: (c, 0))

    low = 1 << (owners.bit_length() - 1) // 2
    length = dict(z=owners // low, x=low, y=shards // 2)
    bit = dict(z=low * shards, x=shards, y=2)
    orders = ("zyx", "yxz", "xyz")

    def turn(rel, which):
        at = dict(
            y=rel % length["y"],
            x=rel // length["y"] % length["x"],
            z=rel // (length["y"] * length["x"]),
        )
        first, second, third = orders[which]
        return (at[first] * length[second] + at[second]) * length[third] + at[third]

    rows_k = -(-latent // devices // 16) * 16
    rows_q = width_q // devices
    shared = rows_q // 64 * 16
    blocks = []
    for rows in (rows_k, rows_k + shared, rows_q - shared):
        shape = (devices // 2, rows, inner)
        blocks += [jax.ShapeDtypeStruct(shape, BF16)] * 2
    spare = rows_k
    context, *blocks = pl.pallas_call(
        functools.partial(
            attend_kernel,
            len(pieces) // shards,
            shards,
            heads,
            scale,
            devices,
            spans,
            turn,
        ),
        grid=(spans,),
        out_shape=[jax.ShapeDtypeStruct((spans * span, inner), BF16)] + blocks,
        in_specs=[HBM] * len(pieces) + [SMEM] + [HBM] * 4,
        out_specs=[by_span] + [VMEM] * len(blocks),
        scratch_shapes=[pltpu.VMEM((keys, inner), BF16)] * 2
        + [pltpu.VMEM((heads * span, keys), F32)] * 2
        + [pltpu.VMEM((heads * span, keys), BF16)] * 2
        + [
            pltpu.VMEM((spans, latent, keys), BF16),
            pltpu.VMEM((spans * span, inner), BF16),
        ]
        + [pltpu.VMEM((spans * keys, inner), BF16)] * 2
        + [pltpu.VMEM((latent + spare, inner), F32)] * 2
        + [pltpu.VMEM((2, 8 * width_q // devices, inner), F32)]
        + [pltpu.VMEM((latent, inner), BF16)] * 2
        + [pltpu.VMEM(normed_t.shape, BF16)]
        + [pltpu.VMEM(queries.shape, BF16)] * 2
        + [
            pltpu.VMEM((shards, *piece.shape), BF16)
            for piece in pieces[:: shards]
        ]
        + [pltpu.SemaphoreType.DMA((6,))],
        compiler_params=pltpu.CompilerParams(vmem_limit_bytes=40 << 20),
        cost_estimate=pl.CostEstimate(
            flops=2 * inner * (4 * spans * keys * (latent + 2 * span) + tokens.size),
            bytes_accessed=12 * (2 * latent + width_q) * inner,
            transcendentals=spans * span * keys * heads,
        ),
    )(*pieces, place, queries, ctx_cotangent, normed_t, weights)

    def travel(sends, axis):
        return [swap(part, k * bit[axis], devices) for k, part in enumerate(sends, 1)]

    keep_v, send_v, keep_p, send_p, keep_r, send_r = blocks
    came_r, came_p, came_v = (swap(s, 1, devices) for s in (send_r, send_p, send_v))
    keep_r, sends = combine([[keep_r, came_r]], length["x"])
    came_r = travel(sends, "x")
    keep_p, sends = combine([[keep_p, came_p]], length["y"], sends[:1])
    came_p = travel(sends, "y")
    keep_v, sends = combine([[keep_v, came_v]], length["z"], sends[:1])
    came_v = travel(sends, "z")
    keep_p, sends = combine([[keep_p, *came_p]], length["x"], came_v[:1])
    came_p = travel(sends, "x")
    keep_r, sends = combine([[keep_r, *came_r]], length["y"], [*sends[:1], *came_v[:2]])
    came_r = travel(sends, "y")
    keep_v, sends = combine([[keep_v, *came_v]], length["y"], sends[:1])
    came_v = travel(sends, "y")
    keep, sends = combine(
        [[keep_p, *came_p], [keep_r, *came_r]], length["z"], sends[:1]
    )
    came = travel(sends, "z")
    keep_v, sends = combine([[keep_v, *came_v]], length["x"], sends[:1])
    came_v = travel(sends, "x")
    ends = [keep_v, *came_v, keep, *came]
    grad_query, grad_key, grad_value = pl.pallas_call(
        functools.partial(finish_kernel, 1 + len(came_v), rows_k),
        out_shape=[
            jax.ShapeDtypeStruct((rows_q, inner), F32),
            jax.ShapeDtypeStruct((latent // devices, inner), F32),
            jax.ShapeDtypeStruct((latent // devices, inner), F32),
        ],
        in_specs=[VMEM] * len(ends),
        out_specs=[VMEM] * 3,
        compiler_params=pltpu.CompilerParams(vmem_limit_bytes=16 << 20),
    )(*ends)
    return context, grad_query, grad_key, grad_value


def solution(mesh):
    rows = P(AXES, None)
    by_shard = P("shard", None)
    return jax.shard_map(
        body,
        mesh=mesh,
        in_specs=(rows, rows, P("dp", "shard", None), rows)
        + (by_shard, by_shard, by_shard),
        out_specs=(rows, rows, rows, rows),
        check_vma=False,
    )
```
